32 devices in a mesh: scan: 4 (over y, x), cross: 8 (over z, core).
Axes of the slice: x: 2, y: 2, z: 4, core: 2. Of those that a mesh axis runs over, the one named last changes fastest.
Arguments:
- wafer_state: float32 [64, 128, 384], P('scan', 'cross'), may hold values from 0 to 1, as said below
- layer_heat_coefficients: float32 [256], replicated, may hold values from 0.03 to 0.14
- beam_profile: float32 [128], replicated, may hold values from 0.25 to 1.75
- beam_start: int32 [4], replicated, may hold values from 0 to 63
- beam_steps: int32 [4], replicated, may hold values from 1 to 64
Outputs:
- annealed: float32 [64, 128, 384], P('scan', 'cross')
The draws below stay inside these ranges and needn't reach their ends.
Inputs may be any that keep to these rules, and one draw needn't show every extreme that they name: `wafer_state`: temperatures lie in 0 to 0.6, acid in 0 to 1, protection in 0.5 to 1.
All inputs are finite; a program needn't handle non-finite values.
Results may differ from the reference program's by a relative error of at most 0.00002.
Values sent between devices are 32-bit elements; how exact they have to be, the bound alone decides.
No kernel may reach another device: no remote copies, remote signals or barrier semaphores. Data moves between devices by JAX's collectives and lax.ppermute only.
A program may use at most 64 MiB of HBM per device.

```python
import math
import jax
import jax.numpy as jnp

DEV_X = 16
RESIST = 64
STEPS = 4
SUBSTEPS = 2
LAYER_BINS_TOTAL = 256
SWEEP_BINS = 64
TRANSVERSE_BINS = 128
HALF_WIDTH = 8


def draw_wafer_state(key, part):
    random_warmth_seed, random_proton_seed, random_guard_seed = jax.random.split(key, 3)
    warmth_grid = 0.6 * jax.random.uniform(random_warmth_seed, (SWEEP_BINS, TRANSVERSE_BINS, LAYER_BINS_TOTAL), jnp.float32)
    acid_fraction = jax.random.uniform(random_proton_seed, (SWEEP_BINS, TRANSVERSE_BINS, RESIST), jnp.float32)
    protected_fraction = 0.5 + 0.5 * jax.random.uniform(random_guard_seed, (SWEEP_BINS, TRANSVERSE_BINS, RESIST), jnp.float32)
    return jnp.concatenate([warmth_grid, acid_fraction, protected_fraction], axis=-1)


def touch_ends(drawn, stream_key, least, top_value):
    place = [jax.random.randint(jax.random.fold_in(stream_key, axis), (), 0, length) for axis, length in enumerate(drawn.shape)]
    widest = drawn.shape.index(max(drawn.shape))
    neighbour = place[:widest] + [(place[widest] + 1) % drawn.shape[widest]] + place[widest + 1:]
    return drawn.at[tuple(place)].set(least).at[tuple(neighbour)].set(top_value)


def setup_inputs(seed: int = 0) -> dict:
    arg_keys = jax.random.split(jax.random.key(seed), 6)
    wafer_state = draw_wafer_state(jax.random.fold_in(arg_keys[5], 71), 0)
    layer_heat_coefficients = jnp.clip(jnp.exp(jax.random.uniform(arg_keys[1], (LAYER_BINS_TOTAL,), jnp.float32, math.log(0.03), math.log(0.14))), 0.03, 0.14)
    beam_profile = jnp.clip(1.0 + 0.15 * jax.random.normal(arg_keys[2], (TRANSVERSE_BINS,), jnp.float32), 0.25, 1.75)
    beam_start = touch_ends(jax.random.randint(arg_keys[3], (STEPS,), 0, SWEEP_BINS), jax.random.fold_in(arg_keys[3], 1), 0, SWEEP_BINS - 1).astype(jnp.int32)
    beam_steps = touch_ends(jax.random.randint(arg_keys[4], (STEPS,), 1, 4 * DEV_X + 1), jax.random.fold_in(arg_keys[4], 1), 1, 4 * DEV_X).astype(jnp.int32)
    return dict(wafer_state=wafer_state, layer_heat_coefficients=layer_heat_coefficients, beam_profile=beam_profile, beam_start=beam_start, beam_steps=beam_steps)


heat_power = 0.5
absorb_depth = 6.0
barrier_energy = 3.0
frequency_multiplier = 0.6
proton_mobility = 0.15


def lateral_heat_current(values, coeffs):
    middle_v = values[1:-1, 1:-1]
    middle_c = coeffs[1:-1, 1:-1]
    flow_sum = jnp.zeros_like(middle_v)
    for other_v, other_c in ((values[2:, 1:-1], coeffs[2:, 1:-1]), (values[:-2, 1:-1], coeffs[:-2, 1:-1]), (values[1:-1, 2:], coeffs[1:-1, 2:]), (values[1:-1, :-2], coeffs[1:-1, :-2])):
        flow_sum = flow_sum + 0.5 * (middle_c + other_c) * (other_v - middle_v)
    return flow_sum


def lower_heat_current(values, coeffs, below_v, below_c):
    upper_v = jnp.concatenate([values[..., :1], values[..., :-1]], axis=-1)
    upper_c = jnp.concatenate([coeffs[..., :1], coeffs[..., :-1]], axis=-1)
    lower_v = jnp.concatenate([values[..., 1:], below_v], axis=-1)
    lower_c = jnp.concatenate([coeffs[..., 1:], below_c], axis=-1)
    return 0.5 * (coeffs + upper_c) * (upper_v - values) + 0.5 * (coeffs + lower_c) * (lower_v - values)


def substep(heated_extent, protected_fraction, layer_heat_coefficients, profile, xcoord, center, spread):
    vertical_cells = layer_heat_coefficients.shape[0]
    polymer_coating = protected_fraction.shape[-1]
    warmth_grid = heated_extent[..., :vertical_cells]
    acid_ext = heated_extent[..., vertical_cells:]
    local_heat_coupling = layer_heat_coefficients / (1.0 + 0.25 * warmth_grid * warmth_grid)
    midpoint_warmth = warmth_grid[1:-1, 1:-1]
    midpoint_heat_ability = local_heat_coupling[1:-1, 1:-1]
    blank_stack_vector = jnp.zeros_like(midpoint_warmth[..., :1])
    heat_current = lateral_heat_current(warmth_grid, local_heat_coupling) + lower_heat_current(midpoint_warmth, midpoint_heat_ability, blank_stack_vector, blank_stack_vector + layer_heat_coefficients[-1])
    depth_level = jnp.arange(vertical_cells, dtype=jnp.float32)
    absorb = jnp.where(depth_level >= polymer_coating, jnp.exp(-(depth_level - polymer_coating) / absorb_depth), 0.0)
    beam_spot = jnp.exp(-jnp.square((xcoord - center) / spread))
    energy_input = heat_power * beam_spot[:, None, None] * profile[None, :, None] * absorb
    updated_warmth = midpoint_warmth + heat_current + energy_input
    polymer_warmth = warmth_grid[..., :polymer_coating]
    spread_proton_site = proton_mobility * polymer_warmth * polymer_warmth / (1.0 + polymer_warmth * polymer_warmth)
    middle_a = acid_ext[1:-1, 1:-1]
    middle_d = spread_proton_site[1:-1, 1:-1]
    new_acid = middle_a + lateral_heat_current(acid_ext, spread_proton_site) + lower_heat_current(middle_a, middle_d, middle_a[..., -1:], middle_d[..., -1:])
    cleavage_rate = frequency_multiplier * jnp.exp(-barrier_energy / (1.0 + midpoint_warmth[..., :polymer_coating]))
    new_protect = protected_fraction * (1.0 - cleavage_rate * middle_a)
    return jnp.concatenate([updated_warmth, new_acid], axis=-1), new_protect


def reference(wafer_state, layer_heat_coefficients, beam_profile, beam_start, beam_steps):
    hot_depth = LAYER_BINS_TOTAL + RESIST
    xcoord = jnp.arange(SWEEP_BINS, dtype=jnp.float32)
    spread = float(HALF_WIDTH)
    for frame_no in range(STEPS):
        for sub_no in range(SUBSTEPS):
            center = (beam_start[frame_no] + sub_no * beam_steps[frame_no]).astype(jnp.float32)
            hot_part = wafer_state[..., :hot_depth]
            heated_extent = jnp.pad(hot_part, ((1, 1), (0, 0), (0, 0)), mode="wrap")
            heated_extent = jnp.pad(heated_extent, ((0, 0), (1, 1), (0, 0)))
            hot_part, protected_fraction = substep(heated_extent, wafer_state[..., hot_depth:], layer_heat_coefficients, beam_profile, xcoord, center, spread)
            wafer_state = jnp.concatenate([hot_part, protected_fraction], axis=-1)
        wafer_state = jnp.roll(wafer_state, -DEV_X, axis=0)
        wafer_state = wafer_state.at[SWEEP_BINS - DEV_X:, :, :LAYER_BINS_TOTAL].set(0.0)
    return wafer_state
```

```python
import jax
import jax.numpy as jnp
from jax import lax
from jax.experimental import pallas as pl
from jax.experimental.pallas import tpu as pltpu
from jax.sharding import PartitionSpec as P

STEPS = 4
SUBSTEPS = 2
HALO = STEPS * SUBSTEPS

heat_power = 0.5
absorb_depth = 6.0
barrier_energy = 3.0
frequency_multiplier = 0.6
proton_mobility = 0.15

SUB = 8
LANE = 128


def pair_swap(size, first, wraps):
    pairs = []
    for low in range(first, size + first, 2):
        high = low + 1
        if high >= size:
            if not wraps:
                continue
            high -= size
        pairs += [(low, high), (high, low)]
    return pairs


def reciprocal(value):
    guess = pl.reciprocal(value, approx=True)
    return guess * (2.0 - value * guess)


def anneal_kernel(
    place,
    beam,
    keep,
    own,
    scan_a,
    scan_b,
    cross_a,
    cross_b,
    coeff_ref,
    bottom_ref,
    dose_ref,
    inside_ref,
    out,
    nat,
    heat,
    cond,
    acid,
    diff,
    left,
):
    rows, cols, _ = own.shape
    wide_rows, tiles, wide_cols, _ = nat.shape
    z_tiles = tiles - 1
    fine = wide_cols // SUB
    resist = (own.shape[2] - z_tiles * LANE) // 2
    lane = lax.broadcasted_iota(jnp.int32, (SUB, LANE), 1)
    last_lane = lane == LANE - 1
    first_lane = lane == 0
    in_resist = lane < resist
    acid_face = jnp.where(lane < resist - 1, 1.0, 0.0).astype(jnp.float32)

    row_a = pl.multiple_of(place[0], SUB)
    row_b = pl.multiple_of(place[1], SUB)
    col_a = pl.multiple_of(place[2], SUB)
    col_b = pl.multiple_of(place[3], SUB)
    for tile in range(tiles):
        width = min(LANE, scan_a.shape[2] - tile * LANE)
        lanes = slice(tile * LANE, tile * LANE + width)
        mid = slice(HALO, HALO + cols)
        nat[HALO : HALO + rows, tile, mid, :] = own[:, :, tile * LANE : (tile + 1) * LANE]
        nat[pl.ds(row_a, HALO), tile, mid, :width] = scan_a[:, :, lanes]
        nat[pl.ds(row_b, HALO), tile, mid, :width] = scan_b[:, :, lanes]
        nat[:, tile, pl.ds(col_a, HALO), :width] = cross_a[:, :, lanes]
        nat[:, tile, pl.ds(col_b, HALO), :width] = cross_b[:, :, lanes]

    def conductivity(square, z):
        return coeff_ref[z] * reciprocal(4.0 + square)

    def mobility(square):
        return 0.5 * proton_mobility - 0.5 * proton_mobility * reciprocal(1.0 + square)

    def load_row(x, carry):
        for y in range(fine):
            at = pl.ds(y, SUB, stride=fine)
            for z in range(z_tiles):
                warm = nat[x, z, at, :]
                heat[x, y * z_tiles + z] = warm
                square = warm * warm
                cond[x, y * z_tiles + z] = conductivity(square, z)
                if z == 0:
                    diff[x, y] = mobility(square)
            acid[x, y] = jnp.where(in_resist, nat[x, z_tiles, at, :], 0.0)
        return carry

    lax.fori_loop(0, wide_rows, load_row, 0)

    def fill(x, carry):
        for y in range(fine):
            left[x, y] = jnp.ones((SUB, LANE), jnp.float32)
        return carry

    lax.fori_loop(0, rows, fill, 0)

    def face(value, other, factor, other_factor):
        return (factor + other_factor) * (other - value)

    def protect_row(x, carry):
        for y in range(fine):
            warm = heat[x + HALO, y * z_tiles]
            rate = frequency_multiplier * jnp.exp(-barrier_energy * reciprocal(1.0 + warm))
            left[x, y] = left[x, y] * (1.0 - rate * acid[x + HALO, y])
        return carry

    def x_faces(x):
        faces = [
            face(heat[x, i], heat[x + 1, i], cond[x, i], cond[x + 1, i])
            for i in range(fine * z_tiles)
        ]
        acid_faces = [
            face(acid[x, y], acid[x + 1, y], diff[x, y], diff[x + 1, y]) for y in range(fine)
        ]
        return faces, acid_faces

    def substep(step):
        def row(x, carry):
            heat_before, acid_before = carry
            heat_after, acid_after = x_faces(x)
            spot = beam[step * wide_rows + x]
            kept = keep[step * wide_rows + x]

            warm = [heat[x, i] for i in range(fine * z_tiles)]
            cnd = [cond[x, i] for i in range(fine * z_tiles)]
            gain = [heat_after[i] - heat_before[i] for i in range(fine * z_tiles)]
            for z in range(z_tiles):
                own_i = [y * z_tiles + z for y in range(fine)]
                faces = []
                for y in range(fine):
                    i = own_i[y]
                    if y + 1 < fine:
                        j = own_i[y + 1]
                        faces.append(face(warm[i], warm[j], cnd[i], cnd[j]))
                    else:
                        j = own_i[0]
                        faces.append(
                            face(
                                warm[i],
                                pltpu.roll(warm[j], SUB - 1, 0),
                                cnd[i],
                                pltpu.roll(cnd[j], SUB - 1, 0),
                            )
                        )
                before = pltpu.roll(faces[-1], 1, 0)
                for y in range(fine):
                    gain[own_i[y]] += faces[y] - before
                    before = faces[y]
            for y in range(fine):
                ids = [y * z_tiles + z for z in range(z_tiles)]
                rolled = [pltpu.roll(warm[i], LANE - 1, 1) for i in ids] + [0.0]
                rolled_c = [pltpu.roll(cnd[i], LANE - 1, 1) for i in ids] + [bottom_ref[...]]
                before = 0.0
                for z, i in enumerate(ids):
                    below = jnp.where(last_lane, rolled[z + 1], rolled[z])
                    below_c = jnp.where(last_lane, rolled_c[z + 1], rolled_c[z])
                    flow = face(warm[i], below, cnd[i], below_c)
                    turned = pltpu.roll(flow, 1, 1)
                    gain[i] += flow - jnp.where(first_lane, before, turned)
                    before = turned
            gain_a = [acid_after[y] - acid_before[y] for y in range(fine)]
            acd = [acid[x, y] for y in range(fine)]
            dif = [diff[x, y] for y in range(fine)]
            faces = [face(acd[y], acd[y + 1], dif[y], dif[y + 1]) for y in range(fine - 1)]
            faces.append(
                face(
                    acd[-1],
                    pltpu.roll(acd[0], SUB - 1, 0),
                    dif[-1],
                    pltpu.roll(dif[0], SUB - 1, 0),
                )
            )
            before = pltpu.roll(faces[-1], 1, 0)
            for y in range(fine):
                gain_a[y] += faces[y] - before
                before = faces[y]
                flow = acid_face * face(
                    acd[y],
                    pltpu.roll(acd[y], LANE - 1, 1),
                    dif[y],
                    pltpu.roll(dif[y], LANE - 1, 1),
                )
                gain_a[y] += flow - pltpu.roll(flow, 1, 1)
                inside = inside_ref[y]
                acid[x, y] = (acd[y] + gain_a[y]) * inside
                held = inside * kept
                for z in range(z_tiles):
                    i = y * z_tiles + z
                    new = (warm[i] + gain[i] + spot * dose_ref[i]) * held
                    heat[x, i] = new
                    square = new * new
                    cond[x, i] = conductivity(square, z)
                    if z == 0:
                        diff[x, y] = mobility(square)
            return heat_after, acid_after

        lax.fori_loop(0, rows, protect_row, 0, unroll=2)
        lax.fori_loop(step + 1, wide_rows - 1 - step, row, x_faces(step))

    for step in range(HALO):
        substep(step)

    def store_row(x, carry):
        for y in range(fine):
            at = pl.ds(y, SUB, stride=fine)
            for z in range(z_tiles):
                nat[x + HALO, z, at, :] = heat[x + HALO, y * z_tiles + z]
            nat[x + HALO, z_tiles, at, :] = jnp.where(
                in_resist, acid[x + HALO, y], pltpu.roll(left[x, y], resist, 1)
            )
        for z in range(z_tiles):
            out[x, :, z * LANE : (z + 1) * LANE] = nat[x + HALO, z, HALO : HALO + cols, :]
        mixed = nat[x + HALO, z_tiles, HALO : HALO + cols, :]
        start = own[x, :, z_tiles * LANE :]
        which = lax.broadcasted_iota(jnp.int32, mixed.shape, 1) < resist
        out[x, :, z_tiles * LANE :] = jnp.where(which, mixed, mixed * start)
        return carry

    lax.fori_loop(0, rows, store_row, 0)


def shards(wafer_state, layer_heat_coefficients, beam_profile, beam_start, beam_steps):
    rows, cols, depth = wafer_state.shape
    deep = layer_heat_coefficients.shape[0]
    resist = (depth - deep) // 2
    hot = deep + resist
    scan_count, cross_count = lax.axis_size("scan"), lax.axis_size("cross")
    scan_pos, cross_pos = lax.axis_index("scan"), lax.axis_index("cross")
    total_x, total_y = rows * scan_count, cols * cross_count
    wide_rows, wide_cols = rows + 2 * HALO, cols + 2 * HALO
    z_tiles = deep // LANE
    fine = wide_cols // SUB
    odd_x, odd_y = scan_pos % 2, cross_pos % 2

    hot_part = wafer_state[..., :hot]
    far_x, far_y = rows - HALO, cols - HALO
    send_a = lax.dynamic_slice_in_dim(hot_part, (1 - odd_x) * far_x, HALO, 0)
    send_b = lax.dynamic_slice_in_dim(hot_part, odd_x * far_x, HALO, 0)
    scan_b = lax.ppermute(send_b, "scan", pair_swap(scan_count, 1, True))
    scan_a = lax.ppermute(send_a, "scan", pair_swap(scan_count, 0, True))
    before = jnp.where(odd_x == 1, scan_a, scan_b)
    after = jnp.where(odd_x == 1, scan_b, scan_a)
    tall = jnp.concatenate([before, hot_part, after], 0)
    send_a = lax.dynamic_slice_in_dim(tall, (1 - odd_y) * far_y, HALO, 1)
    send_b = lax.dynamic_slice_in_dim(tall, odd_y * far_y, HALO, 1)
    cross_b = lax.ppermute(send_b, "cross", pair_swap(cross_count, 1, False))
    cross_a = lax.ppermute(send_a, "cross", pair_swap(cross_count, 0, False))

    place = jnp.stack(
        [
            (1 - odd_x) * (rows + HALO),
            odd_x * (rows + HALO),
            (1 - odd_y) * (cols + HALO),
            odd_y * (cols + HALO),
        ]
    ).astype(jnp.int32)

    near = jnp.arange(wide_rows, dtype=jnp.int32) - HALO
    spread = float(rows // 2)
    beam, keep = [], []
    for frame in range(STEPS):
        block = jnp.mod(scan_pos - frame, scan_count)
        xcoord = jnp.mod(block * rows + near, total_x)
        kept = jnp.where(xcoord < rows, 0.0, 1.0)
        for sub in range(SUBSTEPS):
            center = (beam_start[frame] + sub * beam_steps[frame]).astype(jnp.float32)
            beam.append(jnp.exp(-jnp.square((xcoord.astype(jnp.float32) - center) / spread)))
            keep.append(kept if sub == SUBSTEPS - 1 else jnp.ones_like(kept))
    beam = jnp.concatenate(beam).astype(jnp.float32)
    keep = jnp.concatenate(keep).astype(jnp.float32)

    def by_column(value):
        value = value.reshape(SUB, fine).T
        return jnp.broadcast_to(value[:, :, None], (fine, SUB, LANE))

    level = jnp.arange(deep, dtype=jnp.float32)
    absorb = jnp.where(level >= resist, jnp.exp(-(level - resist) / absorb_depth), 0.0)
    profile = lax.dynamic_slice_in_dim(
        jnp.pad(beam_profile, (HALO, HALO)), cross_pos * cols, wide_cols
    )
    dose = by_column(heat_power * profile)[:, None] * absorb.reshape(z_tiles, 1, LANE)
    dose = dose.reshape(fine * z_tiles, SUB, LANE)
    places = jnp.arange(wide_cols, dtype=jnp.int32) - HALO + cross_pos * cols
    inside = by_column(jnp.where((places >= 0) & (places < total_y), 1.0, 0.0).astype(jnp.float32))
    coeff = jnp.broadcast_to(
        (2.0 * layer_heat_coefficients).reshape(z_tiles, 1, LANE), (z_tiles, SUB, LANE)
    )
    bottom = jnp.broadcast_to(0.5 * layer_heat_coefficients[-1], (SUB, LANE))

    smem = pl.BlockSpec(memory_space=pltpu.SMEM)
    vmem = pl.BlockSpec(memory_space=pltpu.VMEM)
    result = pl.pallas_call(
        anneal_kernel,
        out_shape=jax.ShapeDtypeStruct(wafer_state.shape, wafer_state.dtype),
        in_specs=[smem] * 3 + [vmem] * 9,
        out_specs=vmem,
        scratch_shapes=[
            pltpu.VMEM((wide_rows, z_tiles + 1, wide_cols, LANE), jnp.float32),
            pltpu.VMEM((wide_rows, fine * z_tiles, SUB, LANE), jnp.float32),
            pltpu.VMEM((wide_rows, fine * z_tiles, SUB, LANE), jnp.float32),
            pltpu.VMEM((wide_rows, fine, SUB, LANE), jnp.float32),
            pltpu.VMEM((wide_rows, fine, SUB, LANE), jnp.float32),
            pltpu.VMEM((rows, fine, SUB, LANE), jnp.float32),
        ],
        compiler_params=pltpu.CompilerParams(vmem_limit_bytes=48 * 2**20),
        name="anneal",
    )(
        place,
        beam,
        keep,
        wafer_state,
        scan_a,
        scan_b,
        cross_a,
        cross_b,
        coeff,
        bottom,
        dose,
        inside,
    )
    lag_blocks = STEPS % scan_count
    if lag_blocks:
        pairs = [(source, (source - lag_blocks) % scan_count) for source in range(scan_count)]
        result = lax.ppermute(result, "scan", pairs)
    return result


def solution(mesh):
    in_specs = (P("scan", "cross", None), P(), P(), P(), P())
    out_specs = P("scan", "cross", None)
    return jax.shard_map(shards, mesh=mesh, in_specs=in_specs, out_specs=out_specs, check_vma=False)
```

```python
import jax
import jax.numpy as jnp
from jax import lax
from jax.experimental import pallas as pl
from jax.experimental.pallas import tpu as pltpu
from jax.sharding import PartitionSpec as P

STEPS = 4
SUBSTEPS = 2
HALO = STEPS * SUBSTEPS
UNROLL = 2

heat_power = 0.5
absorb_depth = 6.0
barrier_energy = 3.0
frequency_multiplier = 0.6
proton_mobility = 0.15

SUB = 8
LANE = 128


def pair_swap(size, first, wraps):
    pairs = []
    for low in range(first, size + first, 2):
        high = low + 1
        if high >= size:
            if not wraps:
                continue
            high -= size
        pairs += [(low, high), (high, low)]
    return pairs


def reciprocal(value):
    return pltpu.reciprocal(value, approx=True)


def anneal_kernel(
    place,
    beam,
    keep,
    own,
    scan_a,
    scan_b,
    cross_a,
    cross_b,
    coeff_ref,
    under_ref,
    dose_ref,
    inside_ref,
    out,
    nat,
    heat,
    cond,
    acid,
    diff,
    soft,
    left,
    part,
    deep,
    flow,
):
    rows, cols, _ = own.shape
    wide_rows, tiles, wide_cols, _ = nat.shape
    pairs = wide_rows // 2
    z_tiles = tiles - 1
    fine = wide_cols // SUB
    resist = (own.shape[2] - z_tiles * LANE) // 2
    edge_cols = {(HALO - 1) % fine, (HALO + cols) % fine}
    lane = lax.broadcasted_iota(jnp.int32, (SUB, LANE), 1)
    last_lane = lane == LANE - 1
    first_lane = lane == 0
    in_first = lane < resist
    acid_face = jnp.where(lane % resist == resist - 1, 0.0, 1.0).astype(jnp.float32)

    def at(side, y, z):
        return (side * fine + y) * z_tiles + z

    def turn(value):
        return pltpu.roll(value, resist, 1)

    row_a = pl.multiple_of(place[0], SUB)
    row_b = pl.multiple_of(place[1], SUB)
    col_a = pl.multiple_of(place[2], SUB)
    col_b = pl.multiple_of(place[3], SUB)
    for tile in range(tiles):
        width = min(LANE, scan_a.shape[2] - tile * LANE)
        lanes = slice(tile * LANE, tile * LANE + width)
        mid = slice(HALO, HALO + cols)
        nat[HALO : HALO + rows, tile, mid, :] = own[:, :, tile * LANE : (tile + 1) * LANE]
        nat[pl.ds(row_a, HALO), tile, mid, :width] = scan_a[:, :, lanes]
        nat[pl.ds(row_b, HALO), tile, mid, :width] = scan_b[:, :, lanes]
        nat[:, tile, pl.ds(col_a, HALO), :width] = cross_a[:, :, lanes]
        nat[:, tile, pl.ds(col_b, HALO), :width] = cross_b[:, :, lanes]

    def conductivity(warm, z):
        return coeff_ref[z] * reciprocal(4.0 + warm * warm)

    def mobility(warm):
        return 0.5 * proton_mobility - 0.5 * proton_mobility * reciprocal(1.0 + warm * warm)

    def load_pair(x, carry):
        row = (x, wide_rows - 1 - x)
        for y in range(fine):
            take = pl.ds(y, SUB, stride=fine)
            for z in range(z_tiles):
                for side in range(2):
                    warm = nat[row[side], z, take, :]
                    heat[x + 1, at(side, y, z)] = warm
                    cond[x + 1, at(side, y, z)] = conductivity(warm, z)
            warm = jnp.where(
                in_first, nat[row[0], 0, take, :], turn(nat[row[1], 0, take, :])
            )
            soft[x + 1, y] = warm
            diff[x + 1, y] = mobility(warm)
            acid[x + 1, y] = jnp.where(
                in_first, nat[row[0], z_tiles, take, :], turn(nat[row[1], z_tiles, take, :])
            )
        return carry

    for ref in (heat, cond, acid, diff, soft):
        for i in range(ref.shape[1]):
            for x in (0, pairs + 2):
                ref[x, i] = jnp.zeros((SUB, LANE), jnp.float32)
    lax.fori_loop(0, pairs, load_pair, 0)

    def fill(x, carry):
        for y in range(fine):
            left[x, y] = jnp.ones((SUB, LANE), jnp.float32)
        return carry

    lax.fori_loop(0, pairs - HALO, fill, 0)

    def face(value, other, factor, other_factor):
        return (factor + other_factor) * (other - value)

    def protect_pair(x, carry):
        for y in range(fine):
            warm = soft[x + HALO + 1, y]
            rate = frequency_multiplier * jnp.exp(-barrier_energy * reciprocal(1.0 + warm))
            left[x, y] = left[x, y] * (1.0 - rate * acid[x + HALO + 1, y])
        return carry

    def window(x):
        return [ref.at[pl.ds(x, UNROLL + 3)] for ref in (heat, cond, acid, diff, soft)]

    def x_faces(near, k):
        heat, cond, acid, diff, _ = near
        faces = [
            face(heat[k, i], heat[k + 1, i], cond[k, i], cond[k + 1, i])
            for i in range(2 * fine * z_tiles)
        ]
        acid_faces = [
            face(acid[k, y], acid[k + 1, y], diff[k, y], diff[k + 1, y]) for y in range(fine)
        ]
        return faces + acid_faces

    def y_gain(value, factor):
        faces = [
            face(value[y], value[y + 1], factor[y], factor[y + 1]) for y in range(fine - 1)
        ]
        faces.append(
            face(
                value[-1],
                pltpu.roll(value[0], SUB - 1, 0),
                factor[-1],
                pltpu.roll(factor[0], SUB - 1, 0),
            )
        )
        before = [pltpu.roll(faces[-1], 1, 0)] + faces[:-1]
        return [after - b for after, b in zip(faces, before)]

    def z_faces(value, factor):
        rolled = [pltpu.roll(v, LANE - 1, 1) for v in value] + [0.0]
        faces = []
        for z in range(z_tiles):
            below = jnp.where(last_lane, rolled[z + 1], rolled[z])
            below_f = under_ref[z] * reciprocal(4.0 + below * below)
            faces.append(face(value[z], below, factor[z], below_f))
        return faces

    def z_gain(faces):
        gain, before = [], 0.0
        for face_flow in faces:
            turned = pltpu.roll(face_flow, 1, 1)
            gain.append(face_flow - jnp.where(first_lane, before, turned))
            before = turned
        return gain

    def substep(step, cooling):
        for i in range(2 * fine * z_tiles):
            j = (i + fine * z_tiles) % (2 * fine * z_tiles)
            heat[pairs + 1, i] = heat[pairs, j]
            cond[pairs + 1, i] = cond[pairs, j]
        for y in range(fine):
            acid[pairs + 1, y] = turn(acid[pairs, y])
            diff[pairs + 1, y] = turn(diff[pairs, y])

        def sink(near, k):
            heat, cond, acid, diff, _ = near
            for side in range(2):
                for y in range(fine):
                    ids = [at(side, y, z) for z in range(z_tiles)]
                    faces = z_faces([heat[k, i] for i in ids], [cond[k, i] for i in ids])
                    for i, value in zip(ids, faces):
                        deep[i] = value
            for y in range(fine):
                acd, dif = acid[k, y], diff[k, y]
                deep[2 * fine * z_tiles + y] = acid_face * face(
                    acd, pltpu.roll(acd, LANE - 1, 1), dif, pltpu.roll(dif, LANE - 1, 1)
                )

        def gather(near, k, x):
            heat, cond, acid, diff, _ = near
            for side in range(2):
                row = x if side == 0 else wide_rows - 1 - x
                spot = beam[step * wide_rows + row]
                warm = [
                    [heat[k, at(side, y, z)] for z in range(z_tiles)] for y in range(fine)
                ]
                cnd = [[cond[k, at(side, y, z)] for z in range(z_tiles)] for y in range(fine)]
                across = [
                    y_gain([w[z] for w in warm], [c[z] for c in cnd]) for z in range(z_tiles)
                ]
                for y in range(fine):
                    down = z_gain([deep[at(side, y, z)] for z in range(z_tiles)])
                    for z in range(z_tiles):
                        new = warm[y][z] + spot * dose_ref[y * z_tiles + z]
                        part[at(side, y, z)] = new + across[z][y] + down[z]
            acd = [acid[k, y] for y in range(fine)]
            dif = [diff[k, y] for y in range(fine)]
            across = y_gain(acd, dif)
            for y in range(fine):
                i = 2 * fine * z_tiles + y
                down = deep[i]
                part[i] = acd[y] + across[y] + (down - pltpu.roll(down, 1, 1))

        def soften(near, k):
            heat, _, _, diff, soft = near
            for y in range(fine):
                warm = jnp.where(
                    in_first, heat[k, at(0, y, 0)], turn(heat[k, at(1, y, 0)])
                )
                soft[k, y] = warm
                diff[k, y] = mobility(warm)

        def finish(near, k, x, before):
            heat, cond, acid, _, _ = near
            after = x_faces(near, k)
            for side in range(2):
                row = x if side == 0 else wide_rows - 1 - x
                kept = keep[step * wide_rows + row]
                for y in range(fine):
                    for z in range(z_tiles):
                        i = at(side, y, z)
                        new = part[i] + (after[i] - before[i])
                        if cooling:
                            new = new * kept
                        if y in edge_cols:
                            new = new * inside_ref[y]
                        heat[k, i] = new
                        cond[k, i] = conductivity(new, z)
            for y in range(fine):
                i = 2 * fine * z_tiles + y
                new = part[i] + (after[i] - before[i])
                if y in edge_cols:
                    new = new * inside_ref[y]
                acid[k, y] = new
            return after

        def some_pairs(number, carry):
            x = begin + number * UNROLL
            near = window(x)
            before = [flow[i] for i in range(flow.shape[0])]
            for ahead in range(UNROLL):
                k = ahead + 1
                before = finish(near, k, x + ahead, before)
                gather(near, k + 1, x + ahead + 1)
                sink(near, k + 2)
                soften(near, k - 1)
            for i, value in enumerate(before):
                flow[i] = value
            return carry

        lax.fori_loop(0, pairs - HALO, protect_pair, 0, unroll=pairs - HALO)
        count = (pairs - 1 - step + UNROLL - 1) // UNROLL
        begin = pairs - count * UNROLL
        first = window(begin)
        sink(first, 1)
        gather(first, 1, begin)
        sink(first, 2)
        for i, value in enumerate(x_faces(first, 0)):
            flow[i] = value
        lax.fori_loop(0, count, some_pairs, 0)
        soften(window(pairs - 1), 1)

    def frame(number, carry):
        for sub in range(SUBSTEPS):
            substep(number * SUBSTEPS + sub, sub == SUBSTEPS - 1)
        return carry

    lax.fori_loop(0, STEPS, frame, 0)

    def store_pair(x, carry):
        row = (x + HALO, wide_rows - 1 - HALO - x)
        for y in range(fine):
            put = pl.ds(y, SUB, stride=fine)
            for side in range(2):
                for z in range(z_tiles):
                    nat[row[side], z, put, :] = heat[x + HALO + 1, at(side, y, z)]
            acd, kept = acid[x + HALO + 1, y], left[x, y]
            nat[row[0], z_tiles, put, :] = jnp.where(in_first, acd, turn(kept))
            nat[row[1], z_tiles, put, :] = jnp.where(in_first, turn(acd), kept)
        for side in range(2):
            here = row[side] - HALO
            for z in range(z_tiles):
                out[here, :, z * LANE : (z + 1) * LANE] = nat[
                    row[side], z, HALO : HALO + cols, :
                ]
            mixed = nat[row[side], z_tiles, HALO : HALO + cols, :]
            start = own[here, :, z_tiles * LANE :]
            which = lax.broadcasted_iota(jnp.int32, mixed.shape, 1) < resist
            out[here, :, z_tiles * LANE :] = jnp.where(which, mixed, mixed * start)
        return carry

    lax.fori_loop(0, pairs - HALO, store_pair, 0)


def shards(wafer_state, layer_heat_coefficients, beam_profile, beam_start, beam_steps):
    rows, cols, depth = wafer_state.shape
    deep = layer_heat_coefficients.shape[0]
    resist = (depth - deep) // 2
    hot = deep + resist
    scan_count, cross_count = lax.axis_size("scan"), lax.axis_size("cross")
    scan_pos, cross_pos = lax.axis_index("scan"), lax.axis_index("cross")
    total_x, total_y = rows * scan_count, cols * cross_count
    wide_rows, wide_cols = rows + 2 * HALO, cols + 2 * HALO
    z_tiles = deep // LANE
    fine = wide_cols // SUB
    pairs = wide_rows // 2
    odd_x, odd_y = scan_pos % 2, cross_pos % 2

    hot_part = wafer_state[..., :hot]
    far_x, far_y = rows - HALO, cols - HALO
    send_a = lax.dynamic_slice_in_dim(hot_part, (1 - odd_x) * far_x, HALO, 0)
    send_b = lax.dynamic_slice_in_dim(hot_part, odd_x * far_x, HALO, 0)
    scan_b = lax.ppermute(send_b, "scan", pair_swap(scan_count, 1, True))
    scan_a = lax.ppermute(send_a, "scan", pair_swap(scan_count, 0, True))
    before = jnp.where(odd_x == 1, scan_a, scan_b)
    after = jnp.where(odd_x == 1, scan_b, scan_a)
    tall = jnp.concatenate([before, hot_part, after], 0)
    send_a = lax.dynamic_slice_in_dim(tall, (1 - odd_y) * far_y, HALO, 1)
    send_b = lax.dynamic_slice_in_dim(tall, odd_y * far_y, HALO, 1)
    cross_b = lax.ppermute(send_b, "cross", pair_swap(cross_count, 1, False))
    cross_a = lax.ppermute(send_a, "cross", pair_swap(cross_count, 0, False))

    place = jnp.stack(
        [
            (1 - odd_x) * (rows + HALO),
            odd_x * (rows + HALO),
            (1 - odd_y) * (cols + HALO),
            odd_y * (cols + HALO),
        ]
    ).astype(jnp.int32)

    near = jnp.arange(wide_rows, dtype=jnp.int32) - HALO
    spread = float(rows // 2)
    beam, keep = [], []
    for frame in range(STEPS):
        block = jnp.mod(scan_pos - frame, scan_count)
        xcoord = jnp.mod(block * rows + near, total_x)
        kept = jnp.where(xcoord < rows, 0.0, 1.0)
        for sub in range(SUBSTEPS):
            center = (beam_start[frame] + sub * beam_steps[frame]).astype(jnp.float32)
            beam.append(jnp.exp(-jnp.square((xcoord.astype(jnp.float32) - center) / spread)))
            keep.append(kept if sub == SUBSTEPS - 1 else jnp.ones_like(kept))
    beam = jnp.concatenate(beam).astype(jnp.float32)
    keep = jnp.concatenate(keep).astype(jnp.float32)

    def by_column(value):
        value = value.reshape(SUB, fine).T
        return jnp.broadcast_to(value[:, :, None], (fine, SUB, LANE))

    level = jnp.arange(deep, dtype=jnp.float32)
    absorb = jnp.where(level >= resist, jnp.exp(-(level - resist) / absorb_depth), 0.0)
    profile = lax.dynamic_slice_in_dim(
        jnp.pad(beam_profile, (HALO, HALO)), cross_pos * cols, wide_cols
    )
    dose = by_column(heat_power * profile)[:, None] * absorb.reshape(z_tiles, 1, LANE)
    dose = dose.reshape(fine * z_tiles, SUB, LANE)
    places = jnp.arange(wide_cols, dtype=jnp.int32) - HALO + cross_pos * cols
    inside = by_column(jnp.where((places >= 0) & (places < total_y), 1.0, 0.0).astype(jnp.float32))
    coeff = jnp.broadcast_to(
        (2.0 * layer_heat_coefficients).reshape(z_tiles, 1, LANE), (z_tiles, SUB, LANE)
    )
    under = jnp.concatenate([layer_heat_coefficients[1:], layer_heat_coefficients[-1:]])
    under = jnp.broadcast_to((2.0 * under).reshape(z_tiles, 1, LANE), (z_tiles, SUB, LANE))

    smem = pl.BlockSpec(memory_space=pltpu.SMEM)
    vmem = pl.BlockSpec(memory_space=pltpu.VMEM)
    result = pl.pallas_call(
        anneal_kernel,
        out_shape=jax.ShapeDtypeStruct(wafer_state.shape, wafer_state.dtype),
        in_specs=[smem] * 3 + [vmem] * 9,
        out_specs=vmem,
        scratch_shapes=[
            pltpu.VMEM((wide_rows, z_tiles + 1, wide_cols, LANE), jnp.float32),
            pltpu.VMEM((pairs + 4, 2 * fine * z_tiles, SUB, LANE), jnp.float32),
            pltpu.VMEM((pairs + 4, 2 * fine * z_tiles, SUB, LANE), jnp.float32),
            pltpu.VMEM((pairs + 4, fine, SUB, LANE), jnp.float32),
            pltpu.VMEM((pairs + 4, fine, SUB, LANE), jnp.float32),
            pltpu.VMEM((pairs + 4, fine, SUB, LANE), jnp.float32),
            pltpu.VMEM((pairs - HALO, fine, SUB, LANE), jnp.float32),
            pltpu.VMEM(((2 * z_tiles + 1) * fine, SUB, LANE), jnp.float32),
            pltpu.VMEM(((2 * z_tiles + 1) * fine, SUB, LANE), jnp.float32),
            pltpu.VMEM(((2 * z_tiles + 1) * fine, SUB, LANE), jnp.float32),
        ],
        compiler_params=pltpu.CompilerParams(vmem_limit_bytes=48 * 2**20),
        name="anneal",
    )(
        place,
        beam,
        keep,
        wafer_state,
        scan_a,
        scan_b,
        cross_a,
        cross_b,
        coeff,
        under,
        dose,
        inside,
    )
    lag_blocks = STEPS % scan_count
    if lag_blocks:
        pairs = [(source, (source - lag_blocks) % scan_count) for source in range(scan_count)]
        result = lax.ppermute(result, "scan", pairs)
    return result


def solution(mesh):
    in_specs = (P("scan", "cross", None), P(), P(), P(), P())
    out_specs = P("scan", "cross", None)
    return jax.shard_map(shards, mesh=mesh, in_specs=in_specs, out_specs=out_specs, check_vma=False)
```

```python
import functools

import jax
import jax.numpy as jnp
from jax import lax
from jax.experimental import pallas as pl
from jax.experimental.pallas import tpu as pltpu
from jax.sharding import PartitionSpec as P

STEPS = 4
SUBSTEPS = 2
HALO = STEPS * SUBSTEPS

heat_power = 0.5
absorb_depth = 6.0
barrier_energy = 3.0
frequency_multiplier = 0.6
proton_mobility = 0.15

SUB = 8
LANE = 128
UNROLL = 2
PAD = UNROLL + 4


def pair_swap(size, first, wraps):
    pairs = []
    for low in range(first, size + first, 2):
        high = low + 1
        if high >= size:
            if not wraps:
                continue
            high -= size
        pairs += [(low, high), (high, low)]
    return pairs


def reciprocal(value):
    return pltpu.reciprocal(value, approx=True)


def turn(value):
    return pltpu.roll(value, value.shape[-1] // 2, value.ndim - 1)


def lanes_of(shape):
    return lax.broadcasted_iota(jnp.int32, shape, len(shape) - 1)


def halves(low, high):
    return jnp.where(lanes_of(low.shape) < LANE // 2, low, turn(high))


def pack_kernel(z_tiles, place, own, scan_a, scan_b, cross_a, cross_b):
    rows, cols, _ = own.shape
    odd_x, odd_y = place[0] % 2, place[1] % 2

    def acid_pair(first, second, span):
        tile = slice(z_tiles * LANE, (z_tiles + 1) * LANE)
        return halves(own[first, span, tile], own[second, span, tile])

    for out, low_end in ((scan_a, 1 - odd_x), (scan_b, odd_x)):
        def row(d):
            return jnp.where(low_end == 1, rows - 1 - d, d)

        for d in range(HALO):
            for z in range(z_tiles):
                out[d * z_tiles + z] = own[row(d), :, z * LANE : (z + 1) * LANE]
        for d in range(HALO // 2):
            out[HALO * z_tiles + d] = acid_pair(row(d), row(d + HALO // 2), slice(None))
    for out, right_end in ((cross_a, 1 - odd_y), (cross_b, odd_y)):
        span = pl.ds(pl.multiple_of(right_end * (cols - HALO), SUB), HALO)
        for x in range(rows):
            for z in range(z_tiles):
                out[x * z_tiles + z] = own[x, span, z * LANE : (z + 1) * LANE]
        for x in range(rows // 2):
            out[rows * z_tiles + x] = acid_pair(x, x + rows // 2, span)


def corner_kernel(z_tiles, place, cross_a, cross_b, corner_a, corner_b):
    rows = cross_a.shape[0] * 2 // (2 * z_tiles + 1)
    odd_x, odd_y = place[0] % 2, place[1] % 2
    half = HALO // 2
    spot = lax.broadcasted_iota(jnp.int32, (SUB, LANE), 0)
    for out, low_end in ((corner_a, 1 - odd_x), (corner_b, odd_x)):
        for right in range(2):

            def tile(i, z):
                x = jnp.where(low_end == 1, rows - i, i - 1)
                if z < z_tiles:
                    index = x * z_tiles + z
                else:
                    index = rows * z_tiles + x % (rows // 2)
                from_a = (odd_y == 1) if right == 0 else (odd_y == 0)
                value = jnp.where(from_a, cross_a[index], cross_b[index])
                if z == z_tiles:
                    value = jnp.where(x >= rows // 2, turn(value), value)
                return value

            def slot(i, z):
                near, far = tile(i, z), tile(HALO - i, z)
                if right:
                    return jnp.where(spot < HALO - i, near, pltpu.roll(far, HALO - i, 0))
                return jnp.where(spot >= i, near, pltpu.roll(far, i, 0))

            base = right * out.shape[0] // 2
            for i in range(1, half + 1):
                for z in range(z_tiles):
                    out[base + (i - 1) * z_tiles + z] = slot(i, z)
            for i in range(1, half + 1, 2):
                out[base + half * z_tiles + (i - 1) // 2] = halves(
                    slot(i, z_tiles), slot(i + 1, z_tiles)
                )


def restored(corner, right, i, z, z_tiles):
    half = HALO // 2
    base = right * corner.shape[0] // 2
    slot = i if i <= half else max(HALO - i, 1)
    if z < z_tiles:
        value = corner[base + (slot - 1) * z_tiles + z]
    else:
        value = corner[base + half * z_tiles + (slot - 1) // 2]
        if slot % 2 == 0:
            value = turn(value)
    if i > half:
        value = pltpu.roll(value, slot if right else HALO - slot, 0)
    return value


def face(value, other, factor, other_factor):
    return (factor + other_factor) * (other - value)


def mobility(warm):
    return 0.5 * proton_mobility - 0.5 * proton_mobility * reciprocal(1.0 + warm * warm)


class Block:
    def __init__(self, sizes, first, state, tables):
        self.rows, self.cols, self.z_tiles, self.fine = sizes
        self.wide_rows = self.rows + 2 * HALO
        self.pairs = self.wide_rows // 2
        self.first = first
        self.heat, self.cond, self.acid, self.diff, self.soft, self.left = state[:6]
        self.part, self.deep, self.flow = state[6:]
        self.spots, self.keeps, self.dose, self.inside, self.coeff, self.under = tables
        lane = lanes_of((SUB, LANE))
        self.last_lane = lane == LANE - 1
        self.first_lane = lane == 0
        resist = LANE // 2
        self.acid_face = jnp.where(lane % resist == resist - 1, 0.0, 1.0).astype(jnp.float32)
        self.edge_cols = {(HALO - 1) % self.fine, (HALO + self.cols) % self.fine}
        self.lines = 2 * self.fine * self.z_tiles

    def at(self, side, y, z):
        return (side * self.fine + y) * self.z_tiles + z

    def conductivity(self, warm, z):
        return self.coeff[z] * reciprocal(4.0 + warm * warm)

    def fill(self, slot, warm, acid):
        for y in range(self.fine):
            for z in range(self.z_tiles):
                for side in range(2):
                    value = warm(side, y, z)
                    self.heat[slot, self.at(side, y, z)] = value
                    self.cond[slot, self.at(side, y, z)] = self.conductivity(value, z)
            self.acid[slot, y] = acid(y)
            value = halves(warm(0, y, 0), warm(1, y, 0))
            self.soft[slot, y] = value
            self.diff[slot, y] = mobility(value)

    def fill_natural(self, slot, nat, x):
        fine, z_tiles = self.fine, self.z_tiles

        def take(side, y, z):
            return nat[side, x, z, pl.ds(y, SUB, stride=fine), :]

        self.fill(slot, take, lambda y: halves(take(0, y, z_tiles), take(1, y, z_tiles)))

    def window(self, x):
        place = pl.ds(x - self.first, UNROLL + 3)
        return [
            ref.at[place]
            for ref in (self.heat, self.cond, self.acid, self.diff, self.soft, self.left)
        ]

    def x_faces(self, near, k):
        heat, cond, acid, diff = near[:4]
        faces = [
            face(heat[k, i], heat[k + 1, i], cond[k, i], cond[k + 1, i])
            for i in range(self.lines)
        ]
        return faces + [
            face(acid[k, y], acid[k + 1, y], diff[k, y], diff[k + 1, y])
            for y in range(self.fine)
        ]

    def y_gain(self, value, factor):
        faces = [
            face(value[y], value[y + 1], factor[y], factor[y + 1])
            for y in range(self.fine - 1)
        ]
        faces.append(
            face(
                value[-1],
                pltpu.roll(value[0], SUB - 1, 0),
                factor[-1],
                pltpu.roll(factor[0], SUB - 1, 0),
            )
        )
        before = [pltpu.roll(faces[-1], 1, 0)] + faces[:-1]
        return [after - b for after, b in zip(faces, before)]

    def z_faces(self, value, factor):
        rolled = [pltpu.roll(v, LANE - 1, 1) for v in value] + [0.0]
        faces = []
        for z in range(self.z_tiles):
            below = jnp.where(self.last_lane, rolled[z + 1], rolled[z])
            below_f = self.under[z] * reciprocal(4.0 + below * below)
            faces.append(face(value[z], below, factor[z], below_f))
        return faces

    def z_gain(self, faces):
        gain, before = [], 0.0
        for value in faces:
            turned = pltpu.roll(value, 1, 1)
            gain.append(value - jnp.where(self.first_lane, before, turned))
            before = turned
        return gain

    def sink(self, near, k):
        heat, cond, acid, diff = near[:4]
        for side in range(2):
            for y in range(self.fine):
                ids = [self.at(side, y, z) for z in range(self.z_tiles)]
                faces = self.z_faces([heat[k, i] for i in ids], [cond[k, i] for i in ids])
                for i, value in zip(ids, faces):
                    self.deep[i] = value
        for y in range(self.fine):
            acd, dif = acid[k, y], diff[k, y]
            self.deep[self.lines + y] = self.acid_face * face(
                acd, pltpu.roll(acd, LANE - 1, 1), dif, pltpu.roll(dif, LANE - 1, 1)
            )

    def gather(self, near, k, x, step):
        heat, cond, acid, diff = near[:4]
        fine, z_tiles = self.fine, self.z_tiles
        for side in range(2):
            row = x if side == 0 else self.wide_rows - 1 - x
            spot = self.spots[pl.ds(step * self.wide_rows + row, 1), :]
            ids = [[self.at(side, y, z) for y in range(fine)] for z in range(z_tiles)]
            across = [
                self.y_gain([heat[k, i] for i in ids[z]], [cond[k, i] for i in ids[z]])
                for z in range(z_tiles)
            ]
            for y in range(fine):
                down = self.z_gain([self.deep[ids[z][y]] for z in range(z_tiles)])
                for z in range(z_tiles):
                    i = ids[z][y]
                    new = heat[k, i] + spot * self.dose[y * z_tiles + z]
                    self.part[i] = new + across[z][y] + down[z]
        acd = [acid[k, y] for y in range(fine)]
        across = self.y_gain(acd, [diff[k, y] for y in range(fine)])
        for y in range(fine):
            i = self.lines + y
            down = self.deep[i]
            self.part[i] = acd[y] + across[y] + (down - pltpu.roll(down, 1, 1))

    def finish(self, near, k, x, step, cooling, before):
        heat, cond, acid, _, soft, left = near
        after = self.x_faces(near, k)
        for y in range(self.fine):
            rate = frequency_multiplier * jnp.exp(
                -barrier_energy * reciprocal(1.0 + soft[k, y])
            )
            left[k, y] = left[k, y] * (1.0 - rate * acid[k, y])
        for side in range(2):
            row = x if side == 0 else self.wide_rows - 1 - x
            if cooling:
                kept = self.keeps[pl.ds(step // SUBSTEPS * self.wide_rows + row, 1), :]
            for y in range(self.fine):
                for z in range(self.z_tiles):
                    i = self.at(side, y, z)
                    new = self.part[i] + (after[i] - before[i])
                    if cooling:
                        new = new * kept
                    if y in self.edge_cols:
                        new = new * self.inside[y]
                    heat[k, i] = new
                    cond[k, i] = self.conductivity(new, z)
        for y in range(self.fine):
            i = self.lines + y
            new = self.part[i] + (after[i] - before[i])
            if y in self.edge_cols:
                new = new * self.inside[y]
            acid[k, y] = new
        return after

    def soften(self, near, k):
        heat, diff, soft = near[0], near[3], near[4]
        for y in range(self.fine):
            warm = halves(heat[k, self.at(0, y, 0)], heat[k, self.at(1, y, 0)])
            soft[k, y] = warm
            diff[k, y] = mobility(warm)

    def substep(self, step, cooling, begin, count):
        first = self.window(begin)
        self.sink(first, 1)
        self.gather(first, 1, begin, step)
        self.sink(first, 2)
        for i, value in enumerate(self.x_faces(first, 0)):
            self.flow[i] = value

        def some_pairs(number, carry):
            x = begin + number * UNROLL
            near = self.window(x)
            before = [self.flow[i] for i in range(self.flow.shape[0])]
            for ahead in range(UNROLL):
                k = ahead + 1
                before = self.finish(near, k, x + ahead, step, cooling, before)
                self.gather(near, k + 1, x + ahead + 1, step)
                self.sink(near, k + 2)
                self.soften(near, k - 1)
            for i, value in enumerate(before):
                self.flow[i] = value
            return carry

        lax.fori_loop(0, count, some_pairs, 0)
        self.soften(self.window(begin + count * UNROLL), 0)


def for_substeps(body):
    def frame(number, carry):
        for sub in range(SUBSTEPS):
            body(number * SUBSTEPS + sub, sub == SUBSTEPS - 1)
        return carry

    lax.fori_loop(0, STEPS, frame, 0)


def make_tables(sizes, mesh_sizes, place, profile, start, steps, coeff, tables, column):
    rows, cols, z_tiles, fine = sizes
    spots, keeps, dose, inside, coeffs, under = tables
    scan_pos, cross_pos = place[0], place[1]
    scan_count, cross_count = mesh_sizes
    total_x, total_y = rows * scan_count, cols * cross_count
    wide_rows, wide_cols = rows + 2 * HALO, cols + 2 * HALO
    spread = float(rows // 2)

    def frame(number, carry):
        block = lax.rem(scan_pos - number + STEPS * scan_count, scan_count)
        x = lax.broadcasted_iota(jnp.int32, (wide_rows, LANE), 0) + (block * rows - HALO)
        x = jnp.where(x < 0, x + total_x, x)
        x = jnp.where(x >= total_x, x - total_x, x)
        place = pl.ds(pl.multiple_of(number * wide_rows, SUB), wide_rows)
        keeps[place, :] = jnp.where(x < rows, 0.0, 1.0).astype(jnp.float32)
        for sub in range(SUBSTEPS):
            center = (start[number] + sub * steps[number]).astype(jnp.float32)
            away = (x.astype(jnp.float32) - center) / spread
            place = pl.multiple_of((number * SUBSTEPS + sub) * wide_rows, SUB)
            spots[pl.ds(place, wide_rows), :] = jnp.exp(-(away * away))
        return carry

    lax.fori_loop(0, STEPS, frame, 0)

    for y in range(wide_cols):
        at = cross_pos * cols + (y - HALO)
        here = jnp.where(
            (at >= 0) & (at < total_y), profile[jnp.clip(at, 0, total_y - 1)], 0.0
        )
        column[pl.ds(y, 1), :] = jnp.full((1, LANE), heat_power * here, jnp.float32)
    lane = lanes_of((SUB, LANE))
    level = lane.astype(jnp.float32)
    resist = LANE // 2
    for z in range(z_tiles):
        depth = level + float(z * LANE)
        absorb = jnp.exp(-(depth - float(resist)) / absorb_depth)
        absorb = jnp.where(depth >= float(resist), absorb, 0.0)
        for y in range(fine):
            dose[y * z_tiles + z] = absorb * column[pl.ds(y, SUB, stride=fine), :]
        here = jnp.broadcast_to(coeff[z : z + 1, :], (SUB, LANE))
        if z + 1 < z_tiles:
            below = jnp.broadcast_to(coeff[z + 1 : z + 2, :], (SUB, LANE))
            below = pltpu.roll(below, LANE - 1, 1)
        else:
            below = here
        coeffs[z] = 2.0 * here
        under[z] = 2.0 * jnp.where(lane == LANE - 1, below, pltpu.roll(here, LANE - 1, 1))
    spot = lax.broadcasted_iota(jnp.int32, (SUB, LANE), 0)
    for y in range(fine):
        at = spot * fine + (y - HALO + cross_pos * cols)
        inside[y] = jnp.where((at >= 0) & (at < total_y), 1.0, 0.0).astype(jnp.float32)


def inner_kernel(
    sizes, mesh_sizes, place, start, steps, profile, coeff, own, cross_a, cross_b, *refs
):
    row_heat, row_acid, row_left, next_heat, next_acid = refs[:5]
    tables, (nat, column), state = refs[5:11], refs[11:13], refs[13:]
    rows, cols, z_tiles, fine = sizes
    make_tables(sizes, mesh_sizes, place, profile, start, steps, coeff, tables, column)
    block = Block(sizes, HALO, state, tables)
    odd_y = place[1] % 2
    mine = block.pairs - HALO
    col_a = pl.multiple_of((1 - odd_y) * (cols + HALO), SUB)
    col_b = pl.multiple_of(odd_y * (cols + HALO), SUB)
    for pair in range(mine):
        for side in range(2):
            x = pair if side == 0 else rows - 1 - pair
            for z in range(z_tiles + 1):
                nat[side, pair, z, HALO : HALO + cols, :] = own[x, :, z * LANE : (z + 1) * LANE]
                for message, column_at in ((cross_a, col_a), (cross_b, col_b)):
                    if z < z_tiles:
                        value = message[x * z_tiles + z]
                    else:
                        value = message[rows * z_tiles + x % (rows // 2)]
                        if x >= rows // 2:
                            value = turn(value)
                    nat[side, pair, z, pl.ds(column_at, HALO), :] = value

    blank = jnp.zeros((SUB, LANE), jnp.float32)
    for ref in (block.heat, block.cond, block.acid, block.diff, block.soft):
        for i in range(ref.shape[1]):
            ref[0, i] = blank

    def load(x, carry):
        block.fill_natural(x + 1, nat, x)
        for y in range(fine):
            block.left[x + 1, y] = jnp.ones((SUB, LANE), jnp.float32)
        return carry

    lax.fori_loop(0, mine, load, 0)

    def step_body(step, cooling):
        for i in range(block.lines):
            j = (i + block.lines // 2) % block.lines
            block.heat[mine + 1, i] = block.heat[mine, j]
            block.cond[mine + 1, i] = block.cond[mine, j]
            row_heat[step, i] = block.heat[step + 1, i]
        for y in range(fine):
            block.acid[mine + 1, y] = turn(block.acid[mine, y])
            block.diff[mine + 1, y] = turn(block.diff[mine, y])
            row_acid[step, y] = block.acid[step + 1, y]
            row_left[step, y] = block.left[step + 1, y]
        for i in range(block.lines):
            next_heat[step, i] = block.heat[step + 2, i]
        for y in range(fine):
            next_acid[step, y] = block.acid[step + 2, y]
        count = (mine - 1 - step + UNROLL - 1) // UNROLL
        block.substep(step, cooling, block.pairs - count * UNROLL, count)

    for_substeps(step_body)


def outer_kernel(
    sizes,
    place,
    own,
    scan_a,
    scan_b,
    corner_a,
    corner_b,
    row_heat,
    row_acid,
    row_left,
    next_heat,
    next_acid,
    *refs,
):
    tables, out, nat, state = refs[:6], refs[6], refs[7], refs[8:]
    rows, cols, z_tiles, fine = sizes
    block = Block(sizes, 0, state, tables)
    odd_x = place[0] % 2
    mine = block.pairs - HALO
    for scan, corner, side in ((scan_a, corner_a, 1 - odd_x), (scan_b, corner_b, odd_x)):
        for d in range(HALO):
            x = HALO - 1 - d
            for z in range(z_tiles + 1):
                if z < z_tiles:
                    value = scan[d * z_tiles + z]
                else:
                    value = scan[HALO * z_tiles + d % (HALO // 2)]
                    if d >= HALO // 2:
                        value = turn(value)
                nat[side, x, z, HALO : HALO + cols, :] = value
                nat[side, x, z, :HALO, :] = restored(corner, 0, d + 1, z, z_tiles)
                nat[side, x, z, HALO + cols :, :] = restored(corner, 1, d + 1, z, z_tiles)

    blank = jnp.zeros((SUB, LANE), jnp.float32)
    for ref in (block.heat, block.cond, block.acid, block.diff, block.soft):
        for i in range(ref.shape[1]):
            ref[0, i] = blank

    def load(x, carry):
        block.fill_natural(x + 1, nat, x)
        return carry

    lax.fori_loop(0, HALO, load, 0)

    def step_body(step, cooling):
        slot = step + HALO + 1
        block.fill(
            slot,
            lambda side, y, z: row_heat[step, block.at(side, y, z)],
            lambda y: row_acid[step, y],
        )
        for y in range(fine):
            block.left[slot, y] = row_left[step, y]
        block.fill(
            slot + 1,
            lambda side, y, z: next_heat[step, block.at(side, y, z)],
            lambda y: next_acid[step, y],
        )
        block.substep(step, cooling, step + 1, HALO // UNROLL)

    for_substeps(step_body)

    def store(pair, carry):
        slot = pair + HALO + 1
        row = (pair, rows - 1 - pair)
        for y in range(fine):
            put = pl.ds(y, SUB, stride=fine)
            for side in range(2):
                for z in range(z_tiles):
                    nat[side, pair, z, put, :] = block.heat[slot, block.at(side, y, z)]
            acd, kept = block.acid[slot, y], block.left[slot, y]
            low = lanes_of(acd.shape) < LANE // 2
            nat[0, pair, z_tiles, put, :] = jnp.where(low, acd, turn(kept))
            nat[1, pair, z_tiles, put, :] = jnp.where(low, turn(acd), kept)
        for side in range(2):
            for z in range(z_tiles):
                out[row[side], :, z * LANE : (z + 1) * LANE] = nat[
                    side, pair, z, HALO : HALO + cols, :
                ]
            mixed = nat[side, pair, z_tiles, HALO : HALO + cols, :]
            begun = own[row[side], :, z_tiles * LANE :]
            low = lanes_of(mixed.shape) < LANE // 2
            out[row[side], :, z_tiles * LANE :] = jnp.where(low, mixed, mixed * begun)
        return carry

    lax.fori_loop(0, mine, store, 0)


def shards(wafer_state, layer_heat_coefficients, beam_profile, beam_start, beam_steps):
    rows, cols, depth = wafer_state.shape
    deep = layer_heat_coefficients.shape[0]
    scan_count, cross_count = lax.axis_size("scan"), lax.axis_size("cross")
    place = jnp.stack([lax.axis_index("scan"), lax.axis_index("cross")]).astype(jnp.int32)
    wide_rows, wide_cols = rows + 2 * HALO, cols + 2 * HALO
    z_tiles = deep // LANE
    fine = wide_cols // SUB
    mine = rows // 2
    sizes = (rows, cols, z_tiles, fine)
    lines = 2 * fine * z_tiles
    smem = pl.BlockSpec(memory_space=pltpu.SMEM)
    vmem = pl.BlockSpec(memory_space=pltpu.VMEM)
    params = pltpu.CompilerParams(vmem_limit_bytes=40 * 2**20)

    def array(*shape):
        return jax.ShapeDtypeStruct(shape, jnp.float32)

    def state(pairs):
        return [
            pltpu.VMEM((pairs + PAD, lines, SUB, LANE), jnp.float32),
            pltpu.VMEM((pairs + PAD, lines, SUB, LANE), jnp.float32),
            pltpu.VMEM((pairs + PAD, fine, SUB, LANE), jnp.float32),
            pltpu.VMEM((pairs + PAD, fine, SUB, LANE), jnp.float32),
            pltpu.VMEM((pairs + PAD, fine, SUB, LANE), jnp.float32),
            pltpu.VMEM((pairs + PAD, fine, SUB, LANE), jnp.float32),
            pltpu.VMEM((lines + fine, SUB, LANE), jnp.float32),
            pltpu.VMEM((lines + fine, SUB, LANE), jnp.float32),
            pltpu.VMEM((lines + fine, SUB, LANE), jnp.float32),
        ]

    scan_message = array(HALO * z_tiles + HALO // 2, cols, LANE)
    cross_message = array(rows * z_tiles + rows // 2, HALO, LANE)
    corner_message = array(HALO * z_tiles + HALO // 2, HALO, LANE)
    scan_a, scan_b, cross_a, cross_b = pl.pallas_call(
        functools.partial(pack_kernel, z_tiles),
        out_shape=(scan_message, scan_message, cross_message, cross_message),
        in_specs=[smem, vmem],
        out_specs=(vmem,) * 4,
        compiler_params=params,
        name="pack",
    )(place, wafer_state)

    cross_b = lax.ppermute(cross_b, "cross", pair_swap(cross_count, 1, False))
    cross_a = lax.ppermute(cross_a, "cross", pair_swap(cross_count, 0, False))
    scan_b = lax.ppermute(scan_b, "scan", pair_swap(scan_count, 1, True))
    scan_a = lax.ppermute(scan_a, "scan", pair_swap(scan_count, 0, True))

    corner_a, corner_b = pl.pallas_call(
        functools.partial(corner_kernel, z_tiles),
        out_shape=(corner_message, corner_message),
        in_specs=[smem, vmem, vmem],
        out_specs=(vmem,) * 2,
        compiler_params=params,
        name="corners",
    )(place, cross_a, cross_b)
    corner_b = lax.ppermute(corner_b, "scan", pair_swap(scan_count, 1, True))
    corner_a = lax.ppermute(corner_a, "scan", pair_swap(scan_count, 0, True))

    row_shapes = (
        array(HALO, lines, SUB, LANE),
        array(HALO, fine, SUB, LANE),
        array(HALO, fine, SUB, LANE),
        array(HALO, lines, SUB, LANE),
        array(HALO, fine, SUB, LANE),
    )
    table_shapes = (
        array(HALO * wide_rows, LANE),
        array(STEPS * wide_rows, LANE),
        array(fine * z_tiles, SUB, LANE),
        array(fine, SUB, LANE),
        array(z_tiles, SUB, LANE),
        array(z_tiles, SUB, LANE),
    )
    inner = pl.pallas_call(
        functools.partial(inner_kernel, sizes, (scan_count, cross_count)),
        out_shape=row_shapes + table_shapes,
        in_specs=[smem] * 4 + [vmem] * 4,
        out_specs=(vmem,) * (len(row_shapes) + len(table_shapes)),
        scratch_shapes=[
            pltpu.VMEM((2, mine, z_tiles + 1, wide_cols, LANE), jnp.float32),
            pltpu.VMEM((wide_cols, LANE), jnp.float32),
        ]
        + state(mine),
        compiler_params=params,
        cost_estimate=pl.CostEstimate(
            flops=50_000_000, bytes_accessed=8_000_000, transcendentals=1_000_000
        ),
        name="inner",
    )(
        place,
        beam_start,
        beam_steps,
        beam_profile,
        layer_heat_coefficients.reshape(z_tiles, LANE),
        wafer_state,
        cross_a,
        cross_b,
    )
    result = pl.pallas_call(
        functools.partial(outer_kernel, sizes),
        out_shape=jax.ShapeDtypeStruct(wafer_state.shape, wafer_state.dtype),
        in_specs=[smem] + [vmem] * (5 + len(inner)),
        out_specs=vmem,
        scratch_shapes=[pltpu.VMEM((2, mine, z_tiles + 1, wide_cols, LANE), jnp.float32)]
        + state(HALO + mine),
        compiler_params=params,
        name="outer",
    )(place, wafer_state, scan_a, scan_b, corner_a, corner_b, *inner)
    lag_blocks = STEPS % scan_count
    if lag_blocks:
        pairs = [(source, (source - lag_blocks) % scan_count) for source in range(scan_count)]
        result = lax.ppermute(result, "scan", pairs)
    return result


def solution(mesh):
    in_specs = (P("scan", "cross", None), P(), P(), P(), P())
    out_specs = P("scan", "cross", None)
    return jax.shard_map(shards, mesh=mesh, in_specs=in_specs, out_specs=out_specs, check_vma=False)
```

```python
import functools
import math

import jax
import jax.numpy as jnp
from jax import lax
from jax.experimental import pallas as pl
from jax.experimental.pallas import tpu as pltpu
from jax.sharding import PartitionSpec as P

STEPS = 4
SUBSTEPS = 2
HALO = STEPS * SUBSTEPS

heat_power = 0.5
absorb_depth = 6.0
barrier_energy = 3.0
frequency_multiplier = 0.6
proton_mobility = 0.15

exponent = -barrier_energy / math.log(2.0)

SUB = 8
LANE = 128


def pair_swap(size, first, wraps):
    pairs = []
    for low in range(first, size + first, 2):
        high = low + 1
        if high >= size:
            if not wraps:
                continue
            high -= size
        pairs += [(low, high), (high, low)]
    return pairs


def reciprocal(value):
    return pltpu.reciprocal(value, approx=True)


def turn(value):
    return pltpu.roll(value, value.shape[-1] // 2, value.ndim - 1)


def lanes_of(shape):
    return lax.broadcasted_iota(jnp.int32, shape, len(shape) - 1)


def halves(low, high):
    return jnp.where(lanes_of(low.shape) < LANE // 2, low, turn(high))


def pack_kernel(z_tiles, place, own, scan_a, scan_b, cross_a, cross_b):
    rows, cols, _ = own.shape
    odd_x, odd_y = place[0] % 2, place[1] % 2

    def acid_pair(first, second, span):
        tile = slice(z_tiles * LANE, (z_tiles + 1) * LANE)
        return halves(own[first, span, tile], own[second, span, tile])

    for out, low_end in ((scan_a, 1 - odd_x), (scan_b, odd_x)):
        def row(d):
            return jnp.where(low_end == 1, rows - 1 - d, d)

        for d in range(HALO):
            for z in range(z_tiles):
                out[d * z_tiles + z] = own[row(d), :, z * LANE : (z + 1) * LANE]
        for d in range(HALO // 2):
            out[HALO * z_tiles + d] = acid_pair(row(d), row(d + HALO // 2), slice(None))
    for out, right_end in ((cross_a, 1 - odd_y), (cross_b, odd_y)):
        span = pl.ds(pl.multiple_of(right_end * (cols - HALO), SUB), HALO)
        for x in range(rows):
            for z in range(z_tiles):
                out[x * z_tiles + z] = own[x, span, z * LANE : (z + 1) * LANE]
        for x in range(rows // 2):
            out[rows * z_tiles + x] = acid_pair(x, x + rows // 2, span)


def corner_kernel(z_tiles, place, cross_a, cross_b, corner_a, corner_b):
    rows = cross_a.shape[0] * 2 // (2 * z_tiles + 1)
    odd_x, odd_y = place[0] % 2, place[1] % 2
    half = HALO // 2
    spot = lax.broadcasted_iota(jnp.int32, (SUB, LANE), 0)
    for out, low_end in ((corner_a, 1 - odd_x), (corner_b, odd_x)):
        for right in range(2):

            def tile(i, z):
                x = jnp.where(low_end == 1, rows - i, i - 1)
                if z < z_tiles:
                    index = x * z_tiles + z
                else:
                    index = rows * z_tiles + x % (rows // 2)
                from_a = (odd_y == 1) if right == 0 else (odd_y == 0)
                value = jnp.where(from_a, cross_a[index], cross_b[index])
                if z == z_tiles:
                    value = jnp.where(x >= rows // 2, turn(value), value)
                return value

            def slot(i, z):
                near, far = tile(i, z), tile(HALO - i, z)
                if right:
                    return jnp.where(spot < HALO - i, near, pltpu.roll(far, HALO - i, 0))
                return jnp.where(spot >= i, near, pltpu.roll(far, i, 0))

            base = right * out.shape[0] // 2
            for i in range(1, half + 1):
                for z in range(z_tiles):
                    out[base + (i - 1) * z_tiles + z] = slot(i, z)
            for i in range(1, half + 1, 2):
                out[base + half * z_tiles + (i - 1) // 2] = halves(
                    slot(i, z_tiles), slot(i + 1, z_tiles)
                )


def restored(corner, right, i, z, z_tiles):
    half = HALO // 2
    base = right * corner.shape[0] // 2
    slot = i if i <= half else max(HALO - i, 1)
    if z < z_tiles:
        value = corner[base + (slot - 1) * z_tiles + z]
    else:
        value = corner[base + half * z_tiles + (slot - 1) // 2]
        if slot % 2 == 0:
            value = turn(value)
    if i > half:
        value = pltpu.roll(value, slot if right else HALO - slot, 0)
    return value


def face(value, other, factor, other_factor):
    return (factor + other_factor) * (other - value)


def mobility(warm):
    return 0.5 * proton_mobility - 0.5 * proton_mobility * reciprocal(1.0 + warm * warm)


class Line:
    def __init__(self, ref, k):
        self.ref, self.k = ref, k
        self.shape = ref.shape[1:]

    def __getitem__(self, i):
        return self.ref[self.k, i]

    def __setitem__(self, i, value):
        self.ref[self.k, i] = value


class Block:
    def __init__(self, sizes, first, state, tables):
        self.rows, self.cols, self.z_tiles, self.fine = sizes
        self.wide_rows = self.rows + 2 * HALO
        self.pairs = self.wide_rows // 2
        self.first = first
        self.state = state[:6]
        self.part, self.deep = state[6:]
        self.spots, self.keeps, self.dose, self.inside, self.coeff, self.under = tables
        lane = lanes_of((SUB, LANE))
        self.last_lane = lane == LANE - 1
        self.first_lane = lane == 0
        resist = LANE // 2
        self.acid_face = jnp.where(lane % resist == resist - 1, 0.0, 1.0).astype(jnp.float32)
        self.edge_cols = {(HALO - 1) % self.fine, (HALO + self.cols) % self.fine}
        self.lines = 2 * self.fine * self.z_tiles

    def at(self, side, y, z):
        return (side * self.fine + y) * self.z_tiles + z

    def conductivity(self, warm, z):
        return self.coeff[z] * reciprocal(4.0 + warm * warm)

    def fill_natural(self, slot, nat, x):
        fine, z_tiles = self.fine, self.z_tiles
        heat, cond, acid, diff, soft, _ = self.state
        for y in range(fine):
            take = pl.ds(y, SUB, stride=fine)
            for z in range(z_tiles):
                for side in range(2):
                    value = nat[side, x, z, take, :]
                    heat[slot, self.at(side, y, z)] = value
                    cond[slot, self.at(side, y, z)] = self.conductivity(value, z)
            acid[slot, y] = frequency_multiplier * halves(
                nat[0, x, z_tiles, take, :], nat[1, x, z_tiles, take, :]
            )
            value = halves(nat[0, x, 0, take, :], nat[1, x, 0, take, :])
            soft[slot, y] = value
            diff[slot, y] = mobility(value)

    def x_faces(self, one, other):
        heat, cond, acid, diff = one[:4]
        heat_o, cond_o, acid_o, diff_o = other[:4]
        faces = [face(heat[i], heat_o[i], cond[i], cond_o[i]) for i in range(self.lines)]
        return faces + [
            face(acid[y], acid_o[y], diff[y], diff_o[y]) for y in range(self.fine)
        ]

    def y_gain(self, value, factor):
        faces = [
            face(value[y], value[y + 1], factor[y], factor[y + 1])
            for y in range(self.fine - 1)
        ]
        faces.append(
            face(
                value[-1],
                pltpu.roll(value[0], SUB - 1, 0),
                factor[-1],
                pltpu.roll(factor[0], SUB - 1, 0),
            )
        )
        before = [pltpu.roll(faces[-1], 1, 0)] + faces[:-1]
        return [after - b for after, b in zip(faces, before)]

    def z_faces(self, value, factor):
        rolled = [pltpu.roll(v, LANE - 1, 1) for v in value] + [0.0]
        faces = []
        for z in range(self.z_tiles):
            below = jnp.where(self.last_lane, rolled[z + 1], rolled[z])
            below_f = self.under[z] * reciprocal(4.0 + below * below)
            faces.append(face(value[z], below, factor[z], below_f))
        return faces

    def z_gain(self, faces):
        gain, before = [], 0.0
        for value in faces:
            turned = pltpu.roll(value, 1, 1)
            gain.append(value - jnp.where(self.first_lane, before, turned))
            before = turned
        return gain

    def sink(self, pair):
        heat, cond, acid, diff = pair[:4]
        for side in range(2):
            for y in range(self.fine):
                ids = [self.at(side, y, z) for z in range(self.z_tiles)]
                faces = self.z_faces([heat[i] for i in ids], [cond[i] for i in ids])
                for i, value in zip(ids, faces):
                    self.deep[i] = value
        for y in range(self.fine):
            acd, dif = acid[y], diff[y]
            self.deep[self.lines + y] = self.acid_face * face(
                acd, pltpu.roll(acd, LANE - 1, 1), dif, pltpu.roll(dif, LANE - 1, 1)
            )

    def gather(self, pair, x, step):
        heat, cond, acid, diff = pair[:4]
        fine, z_tiles = self.fine, self.z_tiles
        for side in range(2):
            row = x if side == 0 else self.wide_rows - 1 - x
            spot = self.spots[pl.ds(step * self.wide_rows + row, 1), :]
            ids = [[self.at(side, y, z) for y in range(fine)] for z in range(z_tiles)]
            across = [
                self.y_gain([heat[i] for i in ids[z]], [cond[i] for i in ids[z]])
                for z in range(z_tiles)
            ]
            for y in range(fine):
                down = self.z_gain([self.deep[ids[z][y]] for z in range(z_tiles)])
                for z in range(z_tiles):
                    i = ids[z][y]
                    new = heat[i] + spot * self.dose[y * z_tiles + z]
                    self.part[i] = new + across[z][y] + down[z]
        acd = [acid[y] for y in range(fine)]
        across = self.y_gain(acd, [diff[y] for y in range(fine)])
        for y in range(fine):
            i = self.lines + y
            down = self.deep[i]
            self.part[i] = acd[y] + across[y] + (down - pltpu.roll(down, 1, 1))

    def finish(self, pair, new_pair, x, step, cooling, before, after):
        _, _, acid, _, soft, left = pair
        new_heat, new_cond, new_acid, _, _, new_left = new_pair
        for y in range(self.fine if x >= HALO else 0):
            rate = jnp.exp2(exponent * reciprocal(1.0 + soft[y]))
            new_left[y] = left[y] * (1.0 - rate * acid[y])
        for side in range(2):
            row = x if side == 0 else self.wide_rows - 1 - x
            if cooling:
                kept = self.keeps[pl.ds(step // SUBSTEPS * self.wide_rows + row, 1), :]
            for y in range(self.fine):
                for z in range(self.z_tiles):
                    i = self.at(side, y, z)
                    new = self.part[i] + (after[i] - before[i])
                    if cooling:
                        new = new * kept
                    if y in self.edge_cols:
                        new = new * self.inside[y]
                    new_heat[i] = new
                    new_cond[i] = self.conductivity(new, z)
        for y in range(self.fine):
            i = self.lines + y
            new = self.part[i] + (after[i] - before[i])
            if y in self.edge_cols:
                new = new * self.inside[y]
            new_acid[y] = new

    def soften(self, pair):
        heat, _, _, diff, soft, _ = pair
        for y in range(self.fine):
            warm = halves(heat[self.at(0, y, 0)], heat[self.at(1, y, 0)])
            soft[y] = warm
            diff[y] = mobility(warm)

    def slots(self, x, number):
        return [[Line(ref, x - self.first + k) for ref in self.state] for k in range(number)]

    def substep(self, step, cooling, begin, old, new):
        number = len(new)
        self.sink(old[1])
        self.gather(old[1], begin, step)
        if number > 1:
            self.sink(old[2])
        before = self.x_faces(old[0], old[1])
        for ahead in range(number):
            k = ahead + 1
            after = self.x_faces(old[k], old[k + 1])
            self.finish(old[k], new[ahead], begin + ahead, step, cooling, before, after)
            self.soften(new[ahead])
            before = after
            if ahead + 1 < number:
                self.gather(old[k + 1], begin + ahead + 1, step)
            if ahead + 2 < number:
                self.sink(old[k + 2])


def make_tables(sizes, mesh_sizes, place, profile, start, steps, coeff, tables, column):
    rows, cols, z_tiles, fine = sizes
    spots, keeps, dose, inside, coeffs, under = tables
    scan_pos, cross_pos = place[0], place[1]
    scan_count, cross_count = mesh_sizes
    total_x, total_y = rows * scan_count, cols * cross_count
    wide_rows, wide_cols = rows + 2 * HALO, cols + 2 * HALO
    spread = float(rows // 2)

    def frame(number, carry):
        block = lax.rem(scan_pos - number + STEPS * scan_count, scan_count)
        x = lax.broadcasted_iota(jnp.int32, (wide_rows, LANE), 0) + (block * rows - HALO)
        x = jnp.where(x < 0, x + total_x, x)
        x = jnp.where(x >= total_x, x - total_x, x)
        place = pl.ds(pl.multiple_of(number * wide_rows, SUB), wide_rows)
        keeps[place, :] = jnp.where(x < rows, 0.0, 1.0).astype(jnp.float32)
        for sub in range(SUBSTEPS):
            center = (start[number] + sub * steps[number]).astype(jnp.float32)
            away = (x.astype(jnp.float32) - center) / spread
            place = pl.multiple_of((number * SUBSTEPS + sub) * wide_rows, SUB)
            spots[pl.ds(place, wide_rows), :] = jnp.exp(-(away * away))
        return carry

    lax.fori_loop(0, STEPS, frame, 0)

    for y in range(wide_cols):
        at = cross_pos * cols + (y - HALO)
        here = jnp.where(
            (at >= 0) & (at < total_y), profile[jnp.clip(at, 0, total_y - 1)], 0.0
        )
        column[pl.ds(y, 1), :] = jnp.full((1, LANE), heat_power * here, jnp.float32)
    lane = lanes_of((SUB, LANE))
    level = lane.astype(jnp.float32)
    resist = LANE // 2
    for z in range(z_tiles):
        depth = level + float(z * LANE)
        absorb = jnp.exp(-(depth - float(resist)) / absorb_depth)
        absorb = jnp.where(depth >= float(resist), absorb, 0.0)
        for y in range(fine):
            dose[y * z_tiles + z] = absorb * column[pl.ds(y, SUB, stride=fine), :]
        here = jnp.broadcast_to(coeff[z : z + 1, :], (SUB, LANE))
        if z + 1 < z_tiles:
            below = jnp.broadcast_to(coeff[z + 1 : z + 2, :], (SUB, LANE))
            below = pltpu.roll(below, LANE - 1, 1)
        else:
            below = here
        coeffs[z] = 2.0 * here
        under[z] = 2.0 * jnp.where(lane == LANE - 1, below, pltpu.roll(here, LANE - 1, 1))
    spot = lax.broadcasted_iota(jnp.int32, (SUB, LANE), 0)
    for y in range(fine):
        at = spot * fine + (y - HALO + cross_pos * cols)
        inside[y] = jnp.where((at >= 0) & (at < total_y), 1.0, 0.0).astype(jnp.float32)


def inner_kernel(
    sizes, mesh_sizes, place, start, steps, profile, coeff, own, cross_a, cross_b, *refs
):
    here, after, tables, refs = refs[:6], refs[6:10], refs[10:16], refs[16:]
    nat, column, state = refs[0], refs[1], refs[2:]
    rows, cols, z_tiles, fine = sizes
    make_tables(sizes, mesh_sizes, place, profile, start, steps, coeff, tables, column)
    block = Block(sizes, HALO, state, tables)
    odd_y = place[1] % 2
    mine = block.pairs - HALO
    col_a = pl.multiple_of((1 - odd_y) * (cols + HALO), SUB)
    col_b = pl.multiple_of(odd_y * (cols + HALO), SUB)
    for pair in range(mine):
        for side in range(2):
            x = pair if side == 0 else rows - 1 - pair
            for z in range(z_tiles + 1):
                nat[side, pair, z, HALO : HALO + cols, :] = own[x, :, z * LANE : (z + 1) * LANE]
                for message, column_at in ((cross_a, col_a), (cross_b, col_b)):
                    if z < z_tiles:
                        value = message[x * z_tiles + z]
                    else:
                        value = message[rows * z_tiles + x % (rows // 2)]
                        if x >= rows // 2:
                            value = turn(value)
                    nat[side, pair, z, pl.ds(column_at, HALO), :] = value

    for pair in range(mine):
        block.fill_natural(pair, nat, pair)
        for y in range(fine):
            block.state[5][pair, y] = jnp.ones((SUB, LANE), jnp.float32)

    for step in range(HALO):
        slots = block.slots(HALO, mine + 1)
        heat, cond, acid, diff, _, _ = slots[mine]
        heat_m, cond_m, acid_m, diff_m, _, _ = slots[mine - 1]
        for i in range(block.lines):
            j = (i + block.lines // 2) % block.lines
            heat[i] = heat_m[j]
            cond[i] = cond_m[j]
        for y in range(fine):
            acid[y] = turn(acid_m[y])
            diff[y] = turn(diff_m[y])
        for out, ref in zip(here, slots[step]):
            for i in range(ref.shape[0]):
                out[step, i] = ref[i]
        for out, ref in zip(after, slots[step + 1]):
            for i in range(ref.shape[0]):
                out[step, i] = ref[i]
        if step + 1 < mine:
            cooling = step % SUBSTEPS == SUBSTEPS - 1
            block.substep(step, cooling, HALO + step + 1, slots[step:], slots[step + 1 : mine])


def outer_kernel(
    sizes,
    place,
    own,
    scan_a,
    scan_b,
    corner_a,
    corner_b,
    *refs,
):
    here, after, tables, out, nat = refs[:6], refs[6:10], refs[10:16], refs[16], refs[17]
    state = refs[18:]
    rows, cols, z_tiles, fine = sizes
    block = Block(sizes, 0, state, tables)
    odd_x = place[0] % 2
    mine = block.pairs - HALO
    for scan, corner, side in ((scan_a, corner_a, 1 - odd_x), (scan_b, corner_b, odd_x)):
        for d in range(HALO):
            x = HALO - 1 - d
            for z in range(z_tiles + 1):
                if z < z_tiles:
                    value = scan[d * z_tiles + z]
                else:
                    value = scan[HALO * z_tiles + d % (HALO // 2)]
                    if d >= HALO // 2:
                        value = turn(value)
                nat[side, x, z, HALO : HALO + cols, :] = value
                nat[side, x, z, :HALO, :] = restored(corner, 0, d + 1, z, z_tiles)
                nat[side, x, z, HALO + cols :, :] = restored(corner, 1, d + 1, z, z_tiles)

    for x in range(HALO):
        block.fill_natural(x, nat, x)

    for step in range(HALO):

        @pl.when(place[0] >= 0)
        def _():
            last = [Line(ref, step) for ref in here]
            beyond = [Line(ref, step) for ref in after]
            near = block.slots(step, HALO + 1)
            cooling = step % SUBSTEPS == SUBSTEPS - 1
            block.substep(step, cooling, step + 1, near[:HALO] + [last, beyond], near[1:])

    for pair in range(mine):
        slot = pair + HALO
        heat, _, acid, _, _, left = block.state
        row = (pair, rows - 1 - pair)
        for y in range(fine):
            put = pl.ds(y, SUB, stride=fine)
            for side in range(2):
                for z in range(z_tiles):
                    nat[side, pair, z, put, :] = heat[slot, block.at(side, y, z)]
            acd, kept = acid[slot, y] * (1.0 / frequency_multiplier), left[slot, y]
            low = lanes_of(acd.shape) < LANE // 2
            nat[0, pair, z_tiles, put, :] = jnp.where(low, acd, turn(kept))
            nat[1, pair, z_tiles, put, :] = jnp.where(low, turn(acd), kept)
        for side in range(2):
            for z in range(z_tiles):
                out[row[side], :, z * LANE : (z + 1) * LANE] = nat[
                    side, pair, z, HALO : HALO + cols, :
                ]
            mixed = nat[side, pair, z_tiles, HALO : HALO + cols, :]
            begun = own[row[side], :, z_tiles * LANE :]
            low = lanes_of(mixed.shape) < LANE // 2
            out[row[side], :, z_tiles * LANE :] = jnp.where(low, mixed, mixed * begun)


def shards(wafer_state, layer_heat_coefficients, beam_profile, beam_start, beam_steps):
    rows, cols, depth = wafer_state.shape
    deep = layer_heat_coefficients.shape[0]
    scan_count, cross_count = lax.axis_size("scan"), lax.axis_size("cross")
    place = jnp.stack([lax.axis_index("scan"), lax.axis_index("cross")]).astype(jnp.int32)
    wide_rows, wide_cols = rows + 2 * HALO, cols + 2 * HALO
    z_tiles = deep // LANE
    fine = wide_cols // SUB
    mine = rows // 2
    sizes = (rows, cols, z_tiles, fine)
    lines = 2 * fine * z_tiles
    smem = pl.BlockSpec(memory_space=pltpu.SMEM)
    vmem = pl.BlockSpec(memory_space=pltpu.VMEM)
    params = pltpu.CompilerParams(vmem_limit_bytes=40 * 2**20)

    def array(*shape):
        return jax.ShapeDtypeStruct(shape, jnp.float32)

    wide = (lines, lines, fine, fine, fine, fine)

    def state(pairs):
        return [pltpu.VMEM((pairs, n, SUB, LANE), jnp.float32) for n in wide] + [
            pltpu.VMEM((lines + fine, SUB, LANE), jnp.float32),
            pltpu.VMEM((lines + fine, SUB, LANE), jnp.float32),
        ]

    scan_message = array(HALO * z_tiles + HALO // 2, cols, LANE)
    cross_message = array(rows * z_tiles + rows // 2, HALO, LANE)
    corner_message = array(HALO * z_tiles + HALO // 2, HALO, LANE)
    scan_a, scan_b, cross_a, cross_b = pl.pallas_call(
        functools.partial(pack_kernel, z_tiles),
        out_shape=(scan_message, scan_message, cross_message, cross_message),
        in_specs=[smem, vmem],
        out_specs=(vmem,) * 4,
        compiler_params=params,
        name="pack",
    )(place, wafer_state)

    cross_b = lax.ppermute(cross_b, "cross", pair_swap(cross_count, 1, False))
    cross_a = lax.ppermute(cross_a, "cross", pair_swap(cross_count, 0, False))
    scan_b = lax.ppermute(scan_b, "scan", pair_swap(scan_count, 1, True))
    scan_a = lax.ppermute(scan_a, "scan", pair_swap(scan_count, 0, True))

    corner_a, corner_b = pl.pallas_call(
        functools.partial(corner_kernel, z_tiles),
        out_shape=(corner_message, corner_message),
        in_specs=[smem, vmem, vmem],
        out_specs=(vmem,) * 2,
        compiler_params=params,
        name="corners",
    )(place, cross_a, cross_b)
    corner_b = lax.ppermute(corner_b, "scan", pair_swap(scan_count, 1, True))
    corner_a = lax.ppermute(corner_a, "scan", pair_swap(scan_count, 0, True))

    row_shapes = tuple(array(HALO, n, SUB, LANE) for n in wide + wide[:4])
    table_shapes = (
        array(HALO * wide_rows, LANE),
        array(STEPS * wide_rows, LANE),
        array(fine * z_tiles, SUB, LANE),
        array(fine, SUB, LANE),
        array(z_tiles, SUB, LANE),
        array(z_tiles, SUB, LANE),
    )
    inner = pl.pallas_call(
        functools.partial(inner_kernel, sizes, (scan_count, cross_count)),
        out_shape=row_shapes + table_shapes,
        in_specs=[smem] * 4 + [vmem] * 4,
        out_specs=(vmem,) * (len(row_shapes) + len(table_shapes)),
        scratch_shapes=[
            pltpu.VMEM((2, mine, z_tiles + 1, wide_cols, LANE), jnp.float32),
            pltpu.VMEM((wide_cols, LANE), jnp.float32),
        ]
        + state(mine + 1),
        compiler_params=params,
        cost_estimate=pl.CostEstimate(
            flops=50_000_000, bytes_accessed=8_000_000, transcendentals=1_000_000
        ),
        name="inner",
    )(
        place,
        beam_start,
        beam_steps,
        beam_profile,
        layer_heat_coefficients.reshape(z_tiles, LANE),
        wafer_state,
        cross_a,
        cross_b,
    )
    result = pl.pallas_call(
        functools.partial(outer_kernel, sizes),
        out_shape=jax.ShapeDtypeStruct(wafer_state.shape, wafer_state.dtype),
        in_specs=[smem] + [vmem] * (5 + len(inner)),
        out_specs=vmem,
        scratch_shapes=[pltpu.VMEM((2, mine, z_tiles + 1, wide_cols, LANE), jnp.float32)]
        + state(HALO + mine),
        compiler_params=params,
        name="outer",
    )(place, wafer_state, scan_a, scan_b, corner_a, corner_b, *inner)
    lag_blocks = STEPS % scan_count
    if lag_blocks:
        pairs = [(source, (source - lag_blocks) % scan_count) for source in range(scan_count)]
        result = lax.ppermute(result, "scan", pairs)
    return result


def solution(mesh):
    in_specs = (P("scan", "cross", None), P(), P(), P(), P())
    out_specs = P("scan", "cross", None)
    return jax.shard_map(shards, mesh=mesh, in_specs=in_specs, out_specs=out_specs, check_vma=False)
```

```python
import functools
import math

import jax
import jax.numpy as jnp
from jax import lax
from jax.experimental import pallas as pl
from jax.experimental.pallas import tpu as pltpu
from jax.sharding import PartitionSpec as P

STEPS = 4
SUBSTEPS = 2
HALO = STEPS * SUBSTEPS

heat_power = 0.5
absorb_depth = 6.0
barrier_energy = 3.0
frequency_multiplier = 0.6
proton_mobility = 0.15

exponent = -barrier_energy / math.log(2.0)

SUB = 8
LANE = 128


def pair_swap(size, first, wraps):
    pairs = []
    for low in range(first, size + first, 2):
        high = low + 1
        if high >= size:
            if not wraps:
                continue
            high -= size
        pairs += [(low, high), (high, low)]
    return pairs


def reciprocal(value):
    return pltpu.reciprocal(value, approx=True)


def turn(value):
    return pltpu.roll(value, value.shape[-1] // 2, value.ndim - 1)


def lanes_of(shape):
    return lax.broadcasted_iota(jnp.int32, shape, len(shape) - 1)


def halves(low, high):
    return jnp.where(lanes_of(low.shape) < LANE // 2, low, turn(high))


def position():
    return lax.axis_index("scan"), lax.axis_index("cross")


def acid_pair(z_tiles, own, first, second, span):
    tile = slice(z_tiles * LANE, (z_tiles + 1) * LANE)
    return halves(own[first, span, tile], own[second, span, tile])


def pack_scan(z_tiles, own, out, low_end):
    rows = own.shape[0]

    def row(d):
        return jnp.where(low_end == 1, rows - 1 - d, d)

    for d in range(HALO):
        for z in range(z_tiles):
            out[d * z_tiles + z] = own[row(d), :, z * LANE : (z + 1) * LANE]
    for d in range(HALO // 2):
        out[HALO * z_tiles + d] = acid_pair(
            z_tiles, own, row(d), row(d + HALO // 2), slice(None)
        )


def first_pack_kernel(z_tiles, own, scan_b):
    pack_scan(z_tiles, own, scan_b, position()[0] % 2)


def second_pack_kernel(z_tiles, own, _, scan_a, cross_a, cross_b):
    rows, cols, _ = own.shape
    odd_x, odd_y = position()[0] % 2, position()[1] % 2
    for out, right_end in ((cross_a, 1 - odd_y), (cross_b, odd_y)):
        span = pl.ds(pl.multiple_of(right_end * (cols - HALO), SUB), HALO)
        for x in range(rows):
            for z in range(z_tiles):
                out[x * z_tiles + z] = own[x, span, z * LANE : (z + 1) * LANE]
        for x in range(rows // 2):
            out[rows * z_tiles + x] = acid_pair(z_tiles, own, x, x + rows // 2, span)
    pack_scan(z_tiles, own, scan_a, 1 - odd_x)


def corner_kernel(z_tiles, cross_a, cross_b, corner_a, corner_b):
    rows = cross_a.shape[0] * 2 // (2 * z_tiles + 1)
    place = position()
    odd_x, odd_y = place[0] % 2, place[1] % 2
    half = HALO // 2
    spot = lax.broadcasted_iota(jnp.int32, (SUB, LANE), 0)
    for out, low_end in ((corner_a, 1 - odd_x), (corner_b, odd_x)):
        for right in range(2):

            def tile(i, z):
                x = jnp.where(low_end == 1, rows - i, i - 1)
                if z < z_tiles:
                    index = x * z_tiles + z
                else:
                    index = rows * z_tiles + x % (rows // 2)
                from_a = (odd_y == 1) if right == 0 else (odd_y == 0)
                value = jnp.where(from_a, cross_a[index], cross_b[index])
                if z == z_tiles:
                    value = jnp.where(x >= rows // 2, turn(value), value)
                return value

            def slot(i, z):
                near, far = tile(i, z), tile(HALO - i, z)
                if right:
                    return jnp.where(spot < HALO - i, near, pltpu.roll(far, HALO - i, 0))
                return jnp.where(spot >= i, near, pltpu.roll(far, i, 0))

            base = right * out.shape[0] // 2
            for i in range(1, half + 1):
                for z in range(z_tiles):
                    out[base + (i - 1) * z_tiles + z] = slot(i, z)
            for i in range(1, half + 1, 2):
                out[base + half * z_tiles + (i - 1) // 2] = halves(
                    slot(i, z_tiles), slot(i + 1, z_tiles)
                )


def restored(corner, right, i, z, z_tiles):
    half = HALO // 2
    base = right * corner.shape[0] // 2
    slot = i if i <= half else max(HALO - i, 1)
    if z < z_tiles:
        value = corner[base + (slot - 1) * z_tiles + z]
    else:
        value = corner[base + half * z_tiles + (slot - 1) // 2]
        if slot % 2 == 0:
            value = turn(value)
    if i > half:
        value = pltpu.roll(value, slot if right else HALO - slot, 0)
    return value


def face(value, other, factor, other_factor):
    return (factor + other_factor) * (other - value)


def mobility(warm):
    return 0.5 * proton_mobility - 0.5 * proton_mobility * reciprocal(1.0 + warm * warm)


class Line:
    def __init__(self, ref, k):
        self.ref, self.k = ref, k
        self.shape = ref.shape[1:]

    def __getitem__(self, i):
        return self.ref[self.k, i]

    def __setitem__(self, i, value):
        self.ref[self.k, i] = value


class Block:
    def __init__(self, sizes, first, state, tables):
        self.rows, self.cols, self.z_tiles, self.fine = sizes
        self.wide_rows = self.rows + 2 * HALO
        self.pairs = self.wide_rows // 2
        self.first = first
        self.state = state[:6]
        self.part, self.deep = state[6:]
        self.spots, self.keeps, self.dose, self.inside, self.coeff, self.under = tables
        lane = lanes_of((SUB, LANE))
        self.last_lane = lane == LANE - 1
        self.first_lane = lane == 0
        resist = LANE // 2
        self.acid_face = jnp.where(lane % resist == resist - 1, 0.0, 1.0).astype(jnp.float32)
        self.edge_cols = {(HALO - 1) % self.fine, (HALO + self.cols) % self.fine}
        self.lines = 2 * self.fine * self.z_tiles

    def at(self, side, y, z):
        return (side * self.fine + y) * self.z_tiles + z

    def conductivity(self, warm, z):
        return self.coeff[z] * reciprocal(4.0 + warm * warm)

    def fill_natural(self, slot, nat, x):
        fine, z_tiles = self.fine, self.z_tiles
        heat, cond, acid, diff, soft, _ = self.state
        for y in range(fine):
            take = pl.ds(y, SUB, stride=fine)
            for z in range(z_tiles):
                for side in range(2):
                    value = nat[side, x, z, take, :]
                    heat[slot, self.at(side, y, z)] = value
                    cond[slot, self.at(side, y, z)] = self.conductivity(value, z)
            acid[slot, y] = frequency_multiplier * halves(
                nat[0, x, z_tiles, take, :], nat[1, x, z_tiles, take, :]
            )
            value = halves(nat[0, x, 0, take, :], nat[1, x, 0, take, :])
            soft[slot, y] = value
            diff[slot, y] = mobility(value)

    def x_faces(self, one, other):
        heat, cond, acid, diff = one[:4]
        heat_o, cond_o, acid_o, diff_o = other[:4]
        faces = [face(heat[i], heat_o[i], cond[i], cond_o[i]) for i in range(self.lines)]
        return faces + [
            face(acid[y], acid_o[y], diff[y], diff_o[y]) for y in range(self.fine)
        ]

    def y_gain(self, value, factor):
        faces = [
            face(value[y], value[y + 1], factor[y], factor[y + 1])
            for y in range(self.fine - 1)
        ]
        faces.append(
            face(
                value[-1],
                pltpu.roll(value[0], SUB - 1, 0),
                factor[-1],
                pltpu.roll(factor[0], SUB - 1, 0),
            )
        )
        before = [pltpu.roll(faces[-1], 1, 0)] + faces[:-1]
        return [after - b for after, b in zip(faces, before)]

    def z_faces(self, value, factor):
        rolled = [pltpu.roll(v, LANE - 1, 1) for v in value] + [0.0]
        faces = []
        for z in range(self.z_tiles):
            below = jnp.where(self.last_lane, rolled[z + 1], rolled[z])
            below_f = self.under[z] * reciprocal(4.0 + below * below)
            faces.append(face(value[z], below, factor[z], below_f))
        return faces

    def z_gain(self, faces):
        gain, before = [], 0.0
        for value in faces:
            turned = pltpu.roll(value, 1, 1)
            gain.append(value - jnp.where(self.first_lane, before, turned))
            before = turned
        return gain

    def sink(self, pair):
        heat, cond, acid, diff = pair[:4]
        for side in range(2):
            for y in range(self.fine):
                ids = [self.at(side, y, z) for z in range(self.z_tiles)]
                faces = self.z_faces([heat[i] for i in ids], [cond[i] for i in ids])
                for i, value in zip(ids, faces):
                    self.deep[i] = value
        for y in range(self.fine):
            acd, dif = acid[y], diff[y]
            self.deep[self.lines + y] = self.acid_face * face(
                acd, pltpu.roll(acd, LANE - 1, 1), dif, pltpu.roll(dif, LANE - 1, 1)
            )

    def gather(self, pair, x, step):
        heat, cond, acid, diff = pair[:4]
        fine, z_tiles = self.fine, self.z_tiles
        for side in range(2):
            row = x if side == 0 else self.wide_rows - 1 - x
            spot = self.spots[pl.ds(step * self.wide_rows + row, 1), :]
            ids = [[self.at(side, y, z) for y in range(fine)] for z in range(z_tiles)]
            across = [
                self.y_gain([heat[i] for i in ids[z]], [cond[i] for i in ids[z]])
                for z in range(z_tiles)
            ]
            for y in range(fine):
                down = self.z_gain([self.deep[ids[z][y]] for z in range(z_tiles)])
                for z in range(z_tiles):
                    i = ids[z][y]
                    new = heat[i] + spot * self.dose[y * z_tiles + z]
                    self.part[i] = new + across[z][y] + down[z]
        acd = [acid[y] for y in range(fine)]
        across = self.y_gain(acd, [diff[y] for y in range(fine)])
        for y in range(fine):
            i = self.lines + y
            down = self.deep[i]
            self.part[i] = acd[y] + across[y] + (down - pltpu.roll(down, 1, 1))

    def finish(self, pair, new_pair, x, step, cooling, before, after):
        _, _, acid, _, soft, left = pair
        new_heat, new_cond, new_acid, _, _, new_left = new_pair
        for y in range(self.fine if x >= HALO else 0):
            rate = jnp.exp2(exponent * reciprocal(1.0 + soft[y]))
            new_left[y] = left[y] * (1.0 - rate * acid[y])
        for side in range(2):
            row = x if side == 0 else self.wide_rows - 1 - x
            if cooling:
                kept = self.keeps[pl.ds(step // SUBSTEPS * self.wide_rows + row, 1), :]
            for y in range(self.fine):
                for z in range(self.z_tiles):
                    i = self.at(side, y, z)
                    new = self.part[i] + (after[i] - before[i])
                    if cooling:
                        new = new * kept
                    if y in self.edge_cols:
                        new = new * self.inside[y]
                    new_heat[i] = new
                    new_cond[i] = self.conductivity(new, z)
        for y in range(self.fine):
            i = self.lines + y
            new = self.part[i] + (after[i] - before[i])
            if y in self.edge_cols:
                new = new * self.inside[y]
            new_acid[y] = new

    def soften(self, pair):
        heat, _, _, diff, soft, _ = pair
        for y in range(self.fine):
            warm = halves(heat[self.at(0, y, 0)], heat[self.at(1, y, 0)])
            soft[y] = warm
            diff[y] = mobility(warm)

    def slots(self, x, number):
        return [[Line(ref, x - self.first + k) for ref in self.state] for k in range(number)]

    def substep(self, step, cooling, begin, old, new):
        number = len(new)
        self.sink(old[1])
        self.gather(old[1], begin, step)
        if number > 1:
            self.sink(old[2])
        before = self.x_faces(old[0], old[1])
        for ahead in range(number):
            k = ahead + 1
            after = self.x_faces(old[k], old[k + 1])
            self.finish(old[k], new[ahead], begin + ahead, step, cooling, before, after)
            self.soften(new[ahead])
            before = after
            if ahead + 1 < number:
                self.gather(old[k + 1], begin + ahead + 1, step)
            if ahead + 2 < number:
                self.sink(old[k + 2])


def make_tables(sizes, mesh_sizes, place, profile, start, steps, coeff, tables, column):
    rows, cols, z_tiles, fine = sizes
    spots, keeps, dose, inside, coeffs, under = tables
    scan_pos, cross_pos = place[0], place[1]
    scan_count, cross_count = mesh_sizes
    total_x, total_y = rows * scan_count, cols * cross_count
    wide_rows, wide_cols = rows + 2 * HALO, cols + 2 * HALO
    spread = float(rows // 2)

    def frame(number, carry):
        block = lax.rem(scan_pos - number + STEPS * scan_count, scan_count)
        x = lax.broadcasted_iota(jnp.int32, (wide_rows, LANE), 0) + (block * rows - HALO)
        x = jnp.where(x < 0, x + total_x, x)
        x = jnp.where(x >= total_x, x - total_x, x)
        place = pl.ds(pl.multiple_of(number * wide_rows, SUB), wide_rows)
        keeps[place, :] = jnp.where(x < rows, 0.0, 1.0).astype(jnp.float32)
        for sub in range(SUBSTEPS):
            center = (start[number] + sub * steps[number]).astype(jnp.float32)
            away = (x.astype(jnp.float32) - center) / spread
            place = pl.multiple_of((number * SUBSTEPS + sub) * wide_rows, SUB)
            spots[pl.ds(place, wide_rows), :] = jnp.exp(-(away * away))
        return carry

    lax.fori_loop(0, STEPS, frame, 0)

    for y in range(wide_cols):
        at = cross_pos * cols + (y - HALO)
        here = jnp.where(
            (at >= 0) & (at < total_y), profile[jnp.clip(at, 0, total_y - 1)], 0.0
        )
        column[pl.ds(y, 1), :] = jnp.full((1, LANE), heat_power * here, jnp.float32)
    lane = lanes_of((SUB, LANE))
    level = lane.astype(jnp.float32)
    resist = LANE // 2
    for z in range(z_tiles):
        depth = level + float(z * LANE)
        absorb = jnp.exp(-(depth - float(resist)) / absorb_depth)
        absorb = jnp.where(depth >= float(resist), absorb, 0.0)
        for y in range(fine):
            dose[y * z_tiles + z] = absorb * column[pl.ds(y, SUB, stride=fine), :]
        here = jnp.broadcast_to(coeff[z : z + 1, :], (SUB, LANE))
        if z + 1 < z_tiles:
            below = jnp.broadcast_to(coeff[z + 1 : z + 2, :], (SUB, LANE))
            below = pltpu.roll(below, LANE - 1, 1)
        else:
            below = here
        coeffs[z] = 2.0 * here
        under[z] = 2.0 * jnp.where(lane == LANE - 1, below, pltpu.roll(here, LANE - 1, 1))
    spot = lax.broadcasted_iota(jnp.int32, (SUB, LANE), 0)
    for y in range(fine):
        at = spot * fine + (y - HALO + cross_pos * cols)
        inside[y] = jnp.where((at >= 0) & (at < total_y), 1.0, 0.0).astype(jnp.float32)


def inner_kernel(
    sizes, mesh_sizes, start, steps, profile, coeff, own, cross_a, cross_b, *refs
):
    here, after, tables, refs = refs[:6], refs[6:10], refs[10:16], refs[16:]
    nat, column, state = refs[0], refs[1], refs[2:]
    rows, cols, z_tiles, fine = sizes
    place = position()
    make_tables(sizes, mesh_sizes, place, profile, start, steps, coeff, tables, column)
    block = Block(sizes, HALO, state, tables)
    odd_y = place[1] % 2
    mine = block.pairs - HALO
    col_a = pl.multiple_of((1 - odd_y) * (cols + HALO), SUB)
    col_b = pl.multiple_of(odd_y * (cols + HALO), SUB)
    for pair in range(mine):
        for side in range(2):
            x = pair if side == 0 else rows - 1 - pair
            for z in range(z_tiles + 1):
                nat[side, pair, z, HALO : HALO + cols, :] = own[x, :, z * LANE : (z + 1) * LANE]
                for message, column_at in ((cross_a, col_a), (cross_b, col_b)):
                    if z < z_tiles:
                        value = message[x * z_tiles + z]
                    else:
                        value = message[rows * z_tiles + x % (rows // 2)]
                        if x >= rows // 2:
                            value = turn(value)
                    nat[side, pair, z, pl.ds(column_at, HALO), :] = value

    for pair in range(mine):
        block.fill_natural(pair, nat, pair)
        for y in range(fine):
            block.state[5][pair, y] = jnp.ones((SUB, LANE), jnp.float32)

    for step in range(HALO):
        slots = block.slots(HALO, mine + 1)
        heat, cond, acid, diff, _, _ = slots[mine]
        heat_m, cond_m, acid_m, diff_m, _, _ = slots[mine - 1]
        for i in range(block.lines):
            j = (i + block.lines // 2) % block.lines
            heat[i] = heat_m[j]
            cond[i] = cond_m[j]
        for y in range(fine):
            acid[y] = turn(acid_m[y])
            diff[y] = turn(diff_m[y])
        for out, ref in zip(here, slots[step]):
            for i in range(ref.shape[0]):
                out[step, i] = ref[i]
        for out, ref in zip(after, slots[step + 1]):
            for i in range(ref.shape[0]):
                out[step, i] = ref[i]
        if step + 1 < mine:
            cooling = step % SUBSTEPS == SUBSTEPS - 1
            block.substep(step, cooling, HALO + step + 1, slots[step:], slots[step + 1 : mine])


def outer_kernel(
    sizes,
    own,
    scan_a,
    scan_b,
    corner_a,
    corner_b,
    *refs,
):
    here, after, tables, out, nat = refs[:6], refs[6:10], refs[10:16], refs[16], refs[17]
    state = refs[18:]
    rows, cols, z_tiles, fine = sizes
    block = Block(sizes, 0, state, tables)
    place = position()
    odd_x = place[0] % 2
    mine = block.pairs - HALO
    for scan, corner, side in ((scan_a, corner_a, 1 - odd_x), (scan_b, corner_b, odd_x)):
        for d in range(HALO):
            x = HALO - 1 - d
            for z in range(z_tiles + 1):
                if z < z_tiles:
                    value = scan[d * z_tiles + z]
                else:
                    value = scan[HALO * z_tiles + d % (HALO // 2)]
                    if d >= HALO // 2:
                        value = turn(value)
                nat[side, x, z, HALO : HALO + cols, :] = value
                nat[side, x, z, :HALO, :] = restored(corner, 0, d + 1, z, z_tiles)
                nat[side, x, z, HALO + cols :, :] = restored(corner, 1, d + 1, z, z_tiles)

    for x in range(HALO):
        block.fill_natural(x, nat, x)

    for step in range(HALO):

        @pl.when(place[0] >= 0)
        def _():
            last = [Line(ref, step) for ref in here]
            beyond = [Line(ref, step) for ref in after]
            near = block.slots(step, HALO + 1)
            cooling = step % SUBSTEPS == SUBSTEPS - 1
            block.substep(step, cooling, step + 1, near[:HALO] + [last, beyond], near[1:])

    for pair in range(mine):
        slot = pair + HALO
        heat, _, acid, _, _, left = block.state
        row = (pair, rows - 1 - pair)
        for y in range(fine):
            put = pl.ds(y, SUB, stride=fine)
            for side in range(2):
                for z in range(z_tiles):
                    nat[side, pair, z, put, :] = heat[slot, block.at(side, y, z)]
            acd, kept = acid[slot, y] * (1.0 / frequency_multiplier), left[slot, y]
            low = lanes_of(acd.shape) < LANE // 2
            nat[0, pair, z_tiles, put, :] = jnp.where(low, acd, turn(kept))
            nat[1, pair, z_tiles, put, :] = jnp.where(low, turn(acd), kept)
        for side in range(2):
            for z in range(z_tiles):
                out[row[side], :, z * LANE : (z + 1) * LANE] = nat[
                    side, pair, z, HALO : HALO + cols, :
                ]
            mixed = nat[side, pair, z_tiles, HALO : HALO + cols, :]
            begun = own[row[side], :, z_tiles * LANE :]
            low = lanes_of(mixed.shape) < LANE // 2
            out[row[side], :, z_tiles * LANE :] = jnp.where(low, mixed, mixed * begun)


def shards(wafer_state, layer_heat_coefficients, beam_profile, beam_start, beam_steps):
    rows, cols, depth = wafer_state.shape
    deep = layer_heat_coefficients.shape[0]
    scan_count, cross_count = lax.axis_size("scan"), lax.axis_size("cross")
    wide_rows, wide_cols = rows + 2 * HALO, cols + 2 * HALO
    z_tiles = deep // LANE
    fine = wide_cols // SUB
    mine = rows // 2
    sizes = (rows, cols, z_tiles, fine)
    lines = 2 * fine * z_tiles
    smem = pl.BlockSpec(memory_space=pltpu.SMEM)
    vmem = pl.BlockSpec(memory_space=pltpu.VMEM)
    params = pltpu.CompilerParams(vmem_limit_bytes=40 * 2**20)

    def array(*shape):
        return jax.ShapeDtypeStruct(shape, jnp.float32)

    wide = (lines, lines, fine, fine, fine, fine)

    def state(pairs):
        return [pltpu.VMEM((pairs, n, SUB, LANE), jnp.float32) for n in wide] + [
            pltpu.VMEM((lines + fine, SUB, LANE), jnp.float32),
            pltpu.VMEM((lines + fine, SUB, LANE), jnp.float32),
        ]

    scan_message = array(HALO * z_tiles + HALO // 2, cols, LANE)
    cross_message = array(rows * z_tiles + rows // 2, HALO, LANE)
    corner_message = array(HALO * z_tiles + HALO // 2, HALO, LANE)
    scan_b = pl.pallas_call(
        functools.partial(first_pack_kernel, z_tiles),
        out_shape=scan_message,
        in_specs=[vmem],
        out_specs=vmem,
        compiler_params=params,
        name="pack_first",
    )(wafer_state)
    scan_a, cross_a, cross_b = pl.pallas_call(
        functools.partial(second_pack_kernel, z_tiles),
        out_shape=(scan_message, cross_message, cross_message),
        in_specs=[vmem, pl.BlockSpec(memory_space=pl.ANY)],
        out_specs=(vmem,) * 3,
        compiler_params=params,
        name="pack_second",
    )(wafer_state, scan_b)

    scan_b = lax.ppermute(scan_b, "scan", pair_swap(scan_count, 1, True))
    cross_b = lax.ppermute(cross_b, "cross", pair_swap(cross_count, 1, False))
    cross_a = lax.ppermute(cross_a, "cross", pair_swap(cross_count, 0, False))
    scan_a = lax.ppermute(scan_a, "scan", pair_swap(scan_count, 0, True))

    corner_a, corner_b = pl.pallas_call(
        functools.partial(corner_kernel, z_tiles),
        out_shape=(corner_message, corner_message),
        in_specs=[vmem, vmem],
        out_specs=(vmem,) * 2,
        compiler_params=params,
        name="corners",
    )(cross_a, cross_b)
    corner_b = lax.ppermute(corner_b, "scan", pair_swap(scan_count, 1, True))
    corner_a = lax.ppermute(corner_a, "scan", pair_swap(scan_count, 0, True))

    row_shapes = tuple(array(HALO, n, SUB, LANE) for n in wide + wide[:4])
    table_shapes = (
        array(HALO * wide_rows, LANE),
        array(STEPS * wide_rows, LANE),
        array(fine * z_tiles, SUB, LANE),
        array(fine, SUB, LANE),
        array(z_tiles, SUB, LANE),
        array(z_tiles, SUB, LANE),
    )
    inner = pl.pallas_call(
        functools.partial(inner_kernel, sizes, (scan_count, cross_count)),
        out_shape=row_shapes + table_shapes,
        in_specs=[smem] * 3 + [vmem] * 4,
        out_specs=(vmem,) * (len(row_shapes) + len(table_shapes)),
        scratch_shapes=[
            pltpu.VMEM((2, mine, z_tiles + 1, wide_cols, LANE), jnp.float32),
            pltpu.VMEM((wide_cols, LANE), jnp.float32),
        ]
        + state(mine + 1),
        compiler_params=params,
        cost_estimate=pl.CostEstimate(
            flops=50_000_000, bytes_accessed=8_000_000, transcendentals=1_000_000
        ),
        name="inner",
    )(
        beam_start,
        beam_steps,
        beam_profile,
        layer_heat_coefficients.reshape(z_tiles, LANE),
        wafer_state,
        cross_a,
        cross_b,
    )
    result = pl.pallas_call(
        functools.partial(outer_kernel, sizes),
        out_shape=jax.ShapeDtypeStruct(wafer_state.shape, wafer_state.dtype),
        in_specs=[vmem] * (5 + len(inner)),
        out_specs=vmem,
        scratch_shapes=[pltpu.VMEM((2, mine, z_tiles + 1, wide_cols, LANE), jnp.float32)]
        + state(HALO + mine),
        compiler_params=params,
        name="outer",
    )(wafer_state, scan_a, scan_b, corner_a, corner_b, *inner)
    lag_blocks = STEPS % scan_count
    if lag_blocks:
        pairs = [(source, (source - lag_blocks) % scan_count) for source in range(scan_count)]
        result = lax.ppermute(result, "scan", pairs)
    return result


def solution(mesh):
    in_specs = (P("scan", "cross", None), P(), P(), P(), P())
    out_specs = P("scan", "cross", None)
    return jax.shard_map(shards, mesh=mesh, in_specs=in_specs, out_specs=out_specs, check_vma=False)
```
